32 devices in a mesh: dp: 4 (over y, x), ctx: 8 (over z, core).
Axes of the slice: x: 2, y: 2, z: 4, core: 2. Of those that a mesh axis runs over, the one named last changes fastest.
Arguments:
- patches: bfloat16 [4, 640, 1024], P('dp', 'ctx'), may hold values from -6 to 6
- vis_index: int32 [4, 640], P('dp', 'ctx'), may hold values from 0 to 784, as said below
- shifts: int32 [4, 3], P('dp'), may hold values from 0 to 6, as said below
- enc_gain: float32 [1024], replicated, may hold values from 0.5 to 1.5
- enc_qkv: bfloat16 [1024, 1536], replicated, may hold values from -64 to 64, as said below
- enc_out: bfloat16 [512, 1024], replicated, may hold values from -0.25 to 0.25
- enc_to_dec: bfloat16 [1024, 512], replicated, may hold values from -0.1875 to 0.1875
- mask_token: float32 [512], replicated, may hold values from -6 to 6
- dec_gain: float32 [512], replicated, may hold values from 0.5 to 1.5
- dec_qkv: bfloat16 [512, 768], replicated, may hold values from -64 to 64, as said below
- dec_out: bfloat16 [256, 512], replicated, may hold values from -0.375 to 0.375
- dec_cot: bfloat16 [4, 6272, 512], P('dp', 'ctx'), may hold values from -6 to 6
Outputs:
- d_patches: bfloat16 [4, 640, 1024], P('dp', 'ctx')
- grad_flat: float32 [3147776], P(('dp', 'ctx'))
The draws below stay inside these ranges and needn't reach their ends.
Inputs may be any that keep to these rules, and one draw needn't show every extreme that they name: `vis_index`: slots j * 80 to (j + 1) * 80 - 1 of a clip belong to time shard j; its live values are distinct token positions of the shard and stand first, the other slots hold 784. Every shard has 40 or more live slots, and every clip has a shard whose 80 slots are all live. `shifts`: column 0 is the offset in time, below 4; columns 1 and 2 are the offsets along rows and columns, below 7. One clip has offsets 3, 6, 6 and another 0, 0, 0. `enc_qkv`: entries of the size of the inverse square root of the input width. `dec_qkv`: entries of the size of the inverse square root of the input width.
All inputs are finite; a program needn't handle non-finite values.
Results may differ from the reference program's by a relative error of at most 0.02.
Values may be sent and summed in bfloat16 or wider, within the bound.
No kernel may reach another device: no remote copies, remote signals or barrier semaphores. Data moves between devices by JAX's collectives and lax.ppermute only.
A program may use at most 128 MiB of HBM per device.

```python
import jax
import jax.numpy as jnp
from jax import lax

D = 1024
EH = 8
HEAD = 64
ED = 512
DH = 4
T_DEV = 4
WT = 4
GRID = 14
SW = 7
VIS_SHARD = 80
LOCAL = 784
CLIPS = 4
VIS_ALL = 640
TOKENS_CLIP = 6272
GRAD_LEN = 3147776
N_CTX = 8


def drawn_weight(key, fan_in, channels):
    subkeys = jax.random.split(key, 1)
    weight = jax.random.normal(subkeys[0], (fan_in, 3 * channels), jnp.float32) * fan_in ** (-0.5)
    return weight.astype(jnp.bfloat16)


def draw_enc_qkv(key, part):
    return drawn_weight(key, D, EH * HEAD)


def draw_dec_qkv(key, part):
    return drawn_weight(key, ED, DH * HEAD)


def draw_vis_index(key, part):
    shard_count = VIS_ALL // VIS_SHARD
    subkeys = jax.random.split(key, 3)

    def shuffle(subkey):
        return jax.random.permutation(subkey, LOCAL)
    order = jax.vmap(shuffle)(jax.random.split(subkeys[0], CLIPS * shard_count))
    order = order.reshape(CLIPS, shard_count, LOCAL)[:, :, :VIS_SHARD]
    counts = jax.random.randint(subkeys[1], (CLIPS, shard_count), VIS_SHARD // 2, VIS_SHARD + 1)
    fullest = jax.random.randint(subkeys[2], (CLIPS, 1), 0, shard_count)
    counts = jnp.where(jnp.arange(shard_count)[None, :] == fullest, VIS_SHARD, counts)
    slots = jnp.arange(VIS_SHARD)[None, None, :]
    chosen = jnp.where(slots < counts[:, :, None], order, LOCAL)
    return chosen.reshape(CLIPS, VIS_ALL).astype(jnp.int32)


def draw_shifts(key, part):
    subkeys = jax.random.split(key, 3)
    time_part = jax.random.randint(subkeys[0], (CLIPS, 1), 0, WT)
    space_part = jax.random.randint(subkeys[1], (CLIPS, 2), 0, SW)
    values = jnp.concatenate([time_part, space_part], 1)
    chosen_row = jax.random.randint(subkeys[2], (), 0, CLIPS)
    row_ids = jnp.arange(CLIPS)[:, None]
    highest = jnp.array([WT - 1, SW - 1, SW - 1])[None, :]
    values = jnp.where(row_ids == chosen_row, highest, values)
    values = jnp.where(row_ids == (chosen_row + 1) % CLIPS, 0, values)
    return values.astype(jnp.int32)


def level_of(own_key, shape, cuts, smallest, high):
    loudness, own = 1.0, jax.random.fold_in(own_key, 6)
    for axis_at, shards_of in cuts:
        steps = jnp.exp(jax.random.uniform(jax.random.fold_in(own, axis_at), (shards_of,), jnp.float32, smallest / len(cuts), high / len(cuts)))
        loudness = loudness * jnp.repeat(steps, shape[axis_at] // shards_of).reshape([-1 if axis == axis_at else 1 for axis in range(len(shape))])
    return loudness


def scatter_about(stream_key, shape, width, reach, cuts=(), held_as=jnp.bfloat16):
    values = jax.random.normal(stream_key, shape, jnp.float32) * width
    if len(cuts) > 0:
        values = level_of(stream_key, shape, cuts, -0.22, 0.18) * values
    return jnp.clip(values, min=-reach, max=reach).astype(held_as)


def setup_inputs(seed: int = 0) -> dict:
    seeds = jax.random.split(jax.random.key(seed), 13)
    patches = scatter_about(seeds[0], (CLIPS, VIS_ALL, D), 1.0, 6.0, ((0, 4), (1, 8)))
    vis_index = draw_vis_index(jax.random.fold_in(seeds[12], 71), 0)
    shifts = draw_shifts(jax.random.fold_in(seeds[12], 71), 0)
    enc_gain = jnp.clip(1.0 + 0.1 * jax.random.normal(seeds[3], (D,), jnp.float32), 0.5, 1.5)
    enc_qkv = draw_enc_qkv(jax.random.fold_in(seeds[12], 71), 0)
    enc_out = scatter_about(seeds[5], (EH * HEAD, D), (EH * HEAD) ** -0.5, 0.25)
    enc_to_dec = scatter_about(seeds[6], (D, ED), D ** -0.5, 0.1875)
    mask_token = scatter_about(seeds[7], (ED,), 1.0, 6.0, (), jnp.float32)
    dec_gain = jnp.clip(1.0 + 0.1 * jax.random.normal(seeds[8], (ED,), jnp.float32), 0.5, 1.5)
    dec_qkv = draw_dec_qkv(jax.random.fold_in(seeds[12], 71), 0)
    dec_out = scatter_about(seeds[10], (DH * HEAD, ED), (DH * HEAD) ** -0.5, 0.375)
    dec_cot = scatter_about(seeds[11], (CLIPS, TOKENS_CLIP, ED), 1.0, 6.0, ((0, 4), (1, 8)))
    return {"patches": patches, "vis_index": vis_index, "shifts": shifts, "enc_gain": enc_gain, "enc_qkv": enc_qkv, "enc_out": enc_out, "enc_to_dec": enc_to_dec, "mask_token": mask_token, "dec_gain": dec_gain, "dec_qkv": dec_qkv, "dec_out": dec_out, "dec_cot": dec_cot}


norm_eps = 1e-06

def layer_norm(inputs, gain):
    values = inputs.astype(jnp.float32)
    center = values - lax.optimization_barrier(jnp.mean(values, axis=-1, keepdims=True))
    spread = lax.optimization_barrier(jnp.mean(center * center, axis=-1, keepdims=True))
    return (center * lax.rsqrt(spread + norm_eps) * gain).astype(jnp.bfloat16)

def softmax_rows(scores):
    highest = lax.optimization_barrier(jnp.max(scores, axis=-1, keepdims=True))
    raised = jnp.exp(scores - highest)
    return (raised / lax.optimization_barrier(jnp.sum(raised, axis=-1, keepdims=True))).astype(jnp.bfloat16)

def enc_project(inputs, gain, weight):
    normed = layer_norm(inputs, gain)
    joined = jnp.dot(normed, weight, preferred_element_type=jnp.float32).astype(jnp.bfloat16)
    channels = weight.shape[1] // 3
    return (joined[:, :channels], joined[:, channels:2 * channels], joined[:, 2 * channels:])

def enc_attend(query, key_all, value_all, live_all):
    query_rows = query.shape[0]
    key_rows = key_all.shape[0]
    head_count = query.shape[1] // HEAD
    query_heads = query.reshape(query_rows, head_count, HEAD).astype(jnp.float32)
    key_heads = key_all.reshape(key_rows, head_count, HEAD).astype(jnp.float32)
    value_heads = value_all.reshape(key_rows, head_count, HEAD).astype(jnp.float32)
    scores = jnp.einsum('rhd,khd->hrk', query_heads, key_heads) * HEAD ** (-0.5)
    scores = jnp.where(live_all[None, None, :] > 0.5, scores, -1e+30)
    weights = softmax_rows(scores)
    mixed = jnp.einsum('hrk,khd->rhd', weights.astype(jnp.float32), value_heads)
    return mixed.reshape(query_rows, -1).astype(jnp.bfloat16)

def enc_finish(inputs, mixed, out_weight, down_weight):
    residual = (inputs.astype(jnp.float32) + jnp.dot(mixed, out_weight, preferred_element_type=jnp.float32)).astype(jnp.bfloat16)
    return jnp.dot(residual, down_weight, preferred_element_type=jnp.float32).astype(jnp.bfloat16)

def build_grid(latent, slot_index, token, token_rows):
    base = jnp.broadcast_to(token.astype(jnp.float32), (token_rows, token.shape[0]))
    return base.at[slot_index].set(latent.astype(jnp.float32), mode='drop').astype(jnp.bfloat16)

def dec_project(dec_grid, gain, weight):
    normed = layer_norm(dec_grid, gain)
    joined = jnp.dot(normed, weight, preferred_element_type=jnp.float32).astype(jnp.bfloat16)
    channels = weight.shape[1] // 3
    return (joined[:, :channels], joined[:, channels:])

def dec_mix(query, pair_ext, dec_grid, offsets, weight):
    cell_count = GRID * GRID
    steps_own = query.shape[0] // cell_count
    channels = query.shape[1]
    window_span = steps_own + WT
    query_ext = jnp.pad(query.reshape(steps_own, cell_count, channels), ((WT, WT), (0, 0), (0, 0)))
    offset = (offsets[0] + WT - 1) % WT + 1 - WT
    slice_start = (offset + WT).astype(jnp.int32)
    query_win = lax.dynamic_slice_in_dim(query_ext, slice_start, window_span, 0)
    pair_win = lax.dynamic_slice_in_dim(pair_ext, slice_start, window_span, 0)
    joined = jnp.concatenate([query_win, pair_win], -1).reshape(window_span, GRID, GRID, 3 * channels)
    joined = jnp.roll(joined, (-offsets[1], -offsets[2]), axis=(1, 2))
    side_count = GRID // SW
    windows = joined.reshape(window_span // WT, WT, side_count, SW, side_count, SW, 3 * channels)
    windows = windows.transpose(0, 2, 4, 1, 3, 5, 6).reshape(-1, WT * SW * SW, 3 * channels)
    head_count = channels // HEAD
    window_count = windows.shape[0]
    token_count = windows.shape[1]
    query_heads = windows[..., :channels].reshape(window_count, token_count, head_count, HEAD).astype(jnp.float32)
    key_heads = windows[..., channels:2 * channels].reshape(window_count, token_count, head_count, HEAD).astype(jnp.float32)
    value_heads = windows[..., 2 * channels:].reshape(window_count, token_count, head_count, HEAD).astype(jnp.float32)
    scores = jnp.einsum('nqhd,nkhd->nhqk', query_heads, key_heads) * HEAD ** (-0.5)
    weights = softmax_rows(scores)
    attended = jnp.einsum('nhqk,nkhd->nqhd', weights.astype(jnp.float32), value_heads).astype(jnp.bfloat16)
    attended = attended.reshape(window_span // WT, side_count, side_count, WT, SW, SW, channels)
    attended = attended.transpose(0, 3, 1, 4, 2, 5, 6).reshape(window_span, GRID, GRID, channels)
    attended = jnp.roll(attended, (offsets[1], offsets[2]), axis=(1, 2)).reshape(window_span, cell_count, channels)
    own_rows = lax.dynamic_slice_in_dim(attended, (-offset).astype(jnp.int32), steps_own, 0).reshape(-1, channels)
    return dec_grid.astype(jnp.float32) + jnp.dot(own_rows, weight, preferred_element_type=jnp.float32)

def assemble(middle, from_left, from_right):
    steps_own = middle.shape[0]
    rim_width = from_left.shape[0]
    total = middle.astype(jnp.float32)
    total = total + jnp.pad(from_left.astype(jnp.float32), ((0, steps_own - rim_width), (0, 0), (0, 0)))
    total = total + jnp.pad(from_right.astype(jnp.float32), ((steps_own - rim_width, 0), (0, 0), (0, 0)))
    return total.astype(jnp.bfloat16)

def flatten(members, length):
    joined = jnp.concatenate([member.astype(jnp.float32).reshape(-1) for member in members])
    return jnp.pad(joined, (0, length - joined.shape[0]))

def reference(patches, vis_index, shifts, enc_gain, enc_qkv, enc_out, enc_to_dec, mask_token, dec_gain, dec_qkv, dec_out, dec_cot):
    cell_count = GRID * GRID

    def one_clip(clip_inputs):
        clip_tokens, clip_index, offsets, clip_cot = clip_inputs
        tokens = clip_tokens.reshape(N_CTX, VIS_SHARD, D)
        slot_index = clip_index.reshape(N_CTX, VIS_SHARD)
        live_all = (clip_index < LOCAL).astype(jnp.bfloat16)
        query, key_own, value_own = jax.vmap(enc_project, (0, None, None))(tokens, enc_gain, enc_qkv)
        key_all = key_own.reshape(VIS_ALL, -1)
        value_all = value_own.reshape(VIS_ALL, -1)

        def attend_one(query_shard):
            return enc_attend(query_shard, key_all, value_all, live_all)
        mixed = lax.map(attend_one, query)
        latent = jax.vmap(enc_finish, (0, 0, None, None))(tokens, mixed, enc_out, enc_to_dec)

        def grid_one(latent_shard, index_shard, token):
            return build_grid(latent_shard, index_shard, token, LOCAL)
        dec_grid = jax.vmap(grid_one, (0, 0, None))(latent, slot_index, mask_token)
        dec_query, dec_pair = jax.vmap(dec_project, (0, None, None))(dec_grid, dec_gain, dec_qkv)
        pair_cube = dec_pair.reshape(N_CTX, T_DEV, cell_count, -1)
        pair_ext = jnp.concatenate([jnp.roll(pair_cube, 1, 0)[:, T_DEV - WT:], pair_cube, jnp.roll(pair_cube, -1, 0)[:, :WT]], 1)
        cotangent = clip_cot.reshape(N_CTX, LOCAL, -1).astype(jnp.float32)

        def mix_back(query_shard, ext_shard, grid_shard, cot_shard):

            def mix_fn(first, second, third, fourth):
                return dec_mix(first, second, third, offsets, fourth)
            outputs, pullback = jax.vjp(mix_fn, query_shard, ext_shard, grid_shard, dec_out)
            return pullback(cot_shard)
        d_query, d_ext, d_grid_mix, d_dout = jax.vmap(mix_back)(dec_query, pair_ext, dec_grid, cotangent)
        from_left = jnp.roll(d_ext[:, T_DEV + WT:], 1, 0)
        from_right = jnp.roll(d_ext[:, :WT], -1, 0)
        d_pair = jax.vmap(assemble)(d_ext[:, WT:T_DEV + WT], from_left, from_right).reshape(N_CTX, LOCAL, -1)

        def dproj_back(grid_shard, cot_query, cot_pair):
            outputs, pullback = jax.vjp(dec_project, grid_shard, dec_gain, dec_qkv)
            return pullback((cot_query, cot_pair))
        d_grid_proj, d_dgain, d_dqkv = jax.vmap(dproj_back)(dec_grid, d_query, d_pair)
        d_grid = (d_grid_mix.astype(jnp.float32) + d_grid_proj.astype(jnp.float32)).astype(jnp.bfloat16)

        def grid_back(latent_shard, index_shard, cot_shard):

            def grid_fn(first, second):
                return build_grid(first, index_shard, second, LOCAL)
            outputs, pullback = jax.vjp(grid_fn, latent_shard, mask_token)
            return pullback(cot_shard)
        d_latent, d_mask = jax.vmap(grid_back)(latent, slot_index, d_grid)

        def finish_back(token_shard, mixed_shard, cot_shard):
            outputs, pullback = jax.vjp(enc_finish, token_shard, mixed_shard, enc_out, enc_to_dec)
            return pullback(cot_shard)
        d_tokens_res, d_mixed, d_eout, d_e2d = jax.vmap(finish_back)(tokens, mixed, d_latent)

        def attend_step(running, shard_inputs):
            query_shard, cot_shard = shard_inputs

            def attend_fn(first, second, third):
                return enc_attend(first, second, third, live_all)
            outputs, pullback = jax.vjp(attend_fn, query_shard, key_all, value_all)
            d_query_shard, d_key_part, d_value_part = pullback(cot_shard)
            return ((running[0] + d_key_part.astype(jnp.float32), running[1] + d_value_part.astype(jnp.float32)), d_query_shard)
        zero_sum = jnp.zeros(key_all.shape, jnp.float32)
        sums, d_query_enc = lax.scan(attend_step, (zero_sum, zero_sum), (query, d_mixed))
        d_key = sums[0].astype(jnp.bfloat16).reshape(N_CTX, VIS_SHARD, -1)
        d_value = sums[1].astype(jnp.bfloat16).reshape(N_CTX, VIS_SHARD, -1)

        def project_back(token_shard, cot_query, cot_key, cot_value):
            outputs, pullback = jax.vjp(enc_project, token_shard, enc_gain, enc_qkv)
            return pullback((cot_query, cot_key, cot_value))
        d_tokens_proj, d_egain, d_eqkv = jax.vmap(project_back)(tokens, d_query_enc, d_key, d_value)
        d_patches = (d_tokens_res.astype(jnp.float32) + d_tokens_proj.astype(jnp.float32)).astype(jnp.bfloat16).reshape(VIS_ALL, D)
        members = (d_egain, d_eqkv, d_eout, d_e2d, d_mask, d_dgain, d_dqkv, d_dout)
        flat_grads = flatten(tuple((lax.optimization_barrier(jnp.sum(member.astype(jnp.float32), axis=0)) for member in members)), GRAD_LEN)
        return (d_patches, flat_grads)
    d_patches, flat_grads = lax.map(one_clip, (patches, vis_index, shifts, dec_cot))
    return (d_patches, lax.optimization_barrier(jnp.sum(flat_grads, axis=0)))
```

```python
import functools

import jax
import jax.numpy as jnp
from jax import lax
from jax.experimental import pallas as pl
from jax.experimental.pallas import tpu as pltpu
from jax.sharding import PartitionSpec as P

HEAD = 64
WT = 4
GRID = 14
SW = 7


norm_eps = 1e-06


def extended(block, sides, width):
    for axis, dim in sides:
        count = lax.axis_size(axis)
        forward = [(i, i + 1) for i in range(count - 1)]
        forward.append((count - 1, 0))
        backward = [(target, source) for source, target in forward]
        low = lax.ppermute(
            lax.slice_in_dim(block, block.shape[dim] - width, None, axis=dim), axis, forward
        )
        high = lax.ppermute(lax.slice_in_dim(block, 0, width, axis=dim), axis, backward)
        block = jnp.concatenate([low, block, high], axis=dim)
    return block


def layer_norm(inputs, gain):
    values = inputs.astype(jnp.float32)
    center = values - jnp.mean(values, axis=-1, keepdims=True)
    spread = jnp.mean(center * center, axis=-1, keepdims=True)
    return (center * lax.rsqrt(spread + norm_eps) * gain).astype(jnp.bfloat16)


def softmax_rows(scores):
    highest = jnp.max(scores, axis=-1, keepdims=True)
    raised = jnp.exp(scores - highest)
    return (raised / jnp.sum(raised, axis=-1, keepdims=True)).astype(jnp.bfloat16)


def enc_project(inputs, gain, weight):
    normed = layer_norm(inputs, gain)
    joined = jnp.dot(normed, weight, preferred_element_type=jnp.float32).astype(jnp.bfloat16)
    channels = weight.shape[1] // 3
    return (joined[:, :channels], joined[:, channels : 2 * channels], joined[:, 2 * channels :])


def enc_attend(query, key_all, value_all, live_all):
    query_rows = query.shape[0]
    key_rows = key_all.shape[0]
    head_count = query.shape[1] // HEAD
    query_heads = query.reshape(query_rows, head_count, HEAD).transpose(1, 0, 2)
    key_heads = key_all.reshape(key_rows, head_count, HEAD).transpose(1, 0, 2)
    value_heads = value_all.reshape(key_rows, head_count, HEAD).transpose(1, 0, 2)
    scores = jnp.einsum(
        "hrd,hkd->hrk", query_heads, key_heads, preferred_element_type=jnp.float32
    ) * HEAD ** (-0.5)
    scores = jnp.where(live_all[None, None, :] > 0.5, scores, -1e30)
    weights = softmax_rows(scores)
    mixed = jnp.einsum("hrk,hkd->hrd", weights, value_heads, preferred_element_type=jnp.float32)
    return mixed.transpose(1, 0, 2).reshape(query_rows, -1).astype(jnp.bfloat16)


def enc_finish(inputs, mixed, out_weight, down_weight):
    residual = (
        inputs.astype(jnp.float32) + jnp.dot(mixed, out_weight, preferred_element_type=jnp.float32)
    ).astype(jnp.bfloat16)
    return jnp.dot(residual, down_weight, preferred_element_type=jnp.float32).astype(jnp.bfloat16)


def build_grid(latent, slot_index, token, token_rows):
    base = jnp.broadcast_to(token, (token_rows, token.shape[0]))
    return base.at[slot_index].set(latent.astype(jnp.float32), mode="drop").astype(jnp.bfloat16)


def dec_project(dec_grid, gain, weight):
    normed = layer_norm(dec_grid, gain)
    joined = jnp.dot(normed, weight, preferred_element_type=jnp.float32).astype(jnp.bfloat16)
    channels = weight.shape[1] // 3
    return (joined[:, :channels], joined[:, channels:])


def dec_mix(query, pair_ext, dec_grid, offsets, weight):
    cell_count = GRID * GRID
    steps_own = query.shape[0] // cell_count
    channels = query.shape[1]
    window_span = steps_own + WT
    query_ext = jnp.pad(query.reshape(steps_own, cell_count, channels), ((WT, WT), (0, 0), (0, 0)))
    offset = (offsets[0] + WT - 1) % WT + 1 - WT
    slice_start = offset + WT
    query_win = lax.dynamic_slice_in_dim(query_ext, slice_start, window_span, 0)
    pair_win = lax.dynamic_slice_in_dim(pair_ext, slice_start, window_span, 0)
    joined = jnp.concatenate([query_win, pair_win], -1).reshape(
        window_span, GRID, GRID, 3 * channels
    )
    joined = jnp.roll(joined, (-offsets[1], -offsets[2]), axis=(1, 2))
    side_count = GRID // SW
    windows = joined.reshape(window_span // WT, WT, side_count, SW, side_count, SW, 3 * channels)
    windows = windows.transpose(0, 2, 4, 1, 3, 5, 6).reshape(-1, WT * SW * SW, 3 * channels)
    head_count = channels // HEAD
    window_count = windows.shape[0]
    token_count = windows.shape[1]
    query_heads = (
        windows[..., :channels]
        .reshape(window_count, token_count, head_count, HEAD)
        .transpose(0, 2, 1, 3)
    )
    key_heads = (
        windows[..., channels : 2 * channels]
        .reshape(window_count, token_count, head_count, HEAD)
        .transpose(0, 2, 1, 3)
    )
    value_heads = (
        windows[..., 2 * channels :]
        .reshape(window_count, token_count, head_count, HEAD)
        .transpose(0, 2, 1, 3)
    )
    scores = jnp.einsum(
        "nhqd,nhkd->nhqk", query_heads, key_heads, preferred_element_type=jnp.float32
    ) * HEAD ** (-0.5)
    weights = softmax_rows(scores)
    attended = jnp.einsum(
        "nhqk,nhkd->nhqd", weights, value_heads, preferred_element_type=jnp.float32
    ).astype(jnp.bfloat16)
    attended = attended.transpose(0, 2, 1, 3)
    attended = attended.reshape(window_span // WT, side_count, side_count, WT, SW, SW, channels)
    attended = attended.transpose(0, 3, 1, 4, 2, 5, 6).reshape(window_span, GRID, GRID, channels)
    attended = jnp.roll(attended, (offsets[1], offsets[2]), axis=(1, 2)).reshape(
        window_span, cell_count, channels
    )
    own_rows = lax.dynamic_slice_in_dim(attended, -offset, steps_own, 0).reshape(-1, channels)
    return dec_grid.astype(jnp.float32) + jnp.dot(
        own_rows, weight, preferred_element_type=jnp.float32
    )


def assemble(middle, from_left, from_right):
    total = middle.astype(jnp.float32)
    total = total + from_left.astype(jnp.float32)
    total = total + from_right.astype(jnp.float32)
    return total.astype(jnp.bfloat16)


def flatten(members):
    joined = jnp.concatenate([member.astype(jnp.float32).reshape(-1) for member in members])
    return joined


def plain_body(
    patches,
    vis_index,
    shifts,
    enc_gain,
    enc_qkv,
    enc_out,
    enc_to_dec,
    mask_token,
    dec_gain,
    dec_qkv,
    dec_out,
    dec_cot,
):
    tokens = patches[0]
    slot_index = vis_index[0]
    offsets = shifts[0]
    token_rows = dec_cot.shape[1]
    cell_count = GRID * GRID
    steps_own = token_rows // cell_count
    live_own = (slot_index < token_rows).astype(jnp.bfloat16)
    (query, key_own, value_own), project_pull = jax.vjp(enc_project, tokens, enc_gain, enc_qkv)
    key_all, value_all, live_all = (
        lax.all_gather(key_own, "ctx", axis=0, tiled=True),
        lax.all_gather(value_own, "ctx", axis=0, tiled=True),
        lax.all_gather(live_own, "ctx", axis=0, tiled=True),
    )

    def attend_fn(first, second, third):
        return enc_attend(first, second, third, live_all)

    mixed, attend_pull = jax.vjp(attend_fn, query, key_all, value_all)
    latent, finish_pull = jax.vjp(enc_finish, tokens, mixed, enc_out, enc_to_dec)

    def grid_fn(first, second):
        return build_grid(first, slot_index, second, token_rows)

    dec_grid, grid_pull = jax.vjp(grid_fn, latent, mask_token)
    (dec_query, dec_pair), dproj_pull = jax.vjp(dec_project, dec_grid, dec_gain, dec_qkv)
    pair_cube = dec_pair.reshape(steps_own, cell_count, dec_pair.shape[1])
    pair_ext = extended(pair_cube, (("ctx", 0),), WT)

    def mix_fn(first, second, third, fourth):
        return dec_mix(first, second, third, offsets, fourth)

    decoded, mix_pull = jax.vjp(mix_fn, dec_query, pair_ext, dec_grid, dec_out)
    d_query, d_ext, d_grid_mix, d_dout = mix_pull(dec_cot[0].astype(jnp.float32))
    rim_grads = jnp.concatenate([d_ext[:WT], d_ext[steps_own + WT :]], 0)
    beside_all = extended(rim_grads, (("ctx", 0),), WT)
    from_left = beside_all[:WT]
    from_right = beside_all[3 * WT :]
    d_pair = assemble(d_ext[WT : steps_own + WT], from_left, from_right).reshape(token_rows, -1)
    d_grid_proj, d_dgain, d_dqkv = dproj_pull((d_query, d_pair))
    d_grid = (d_grid_mix.astype(jnp.float32) + d_grid_proj.astype(jnp.float32)).astype(jnp.bfloat16)
    d_latent, d_mask = grid_pull(d_grid)
    d_tokens_res, d_mixed, d_eout, d_e2d = finish_pull(d_latent)
    d_query_enc, d_key_all, d_value_all = attend_pull(d_mixed)
    d_key, d_value = (
        lax.psum_scatter(
            d_key_all.astype(jnp.float32).astype(jnp.bfloat16),
            "ctx",
            scatter_dimension=0,
            tiled=True,
        ).astype(jnp.float32),
        lax.psum_scatter(
            d_value_all.astype(jnp.float32).astype(jnp.bfloat16),
            "ctx",
            scatter_dimension=0,
            tiled=True,
        ).astype(jnp.float32),
    )
    d_tokens_proj, d_egain, d_eqkv = project_pull(
        (d_query_enc, d_key.astype(jnp.bfloat16), d_value.astype(jnp.bfloat16))
    )
    d_patches = (d_tokens_res.astype(jnp.float32) + d_tokens_proj.astype(jnp.float32)).astype(
        jnp.bfloat16
    )[None]
    flat_grads = flatten((d_egain, d_eqkv, d_eout, d_e2d, d_mask, d_dgain, d_dqkv, d_dout))
    clip_share = lax.psum_scatter(
        flat_grads.astype(jnp.bfloat16), "dp", scatter_dimension=0, tiled=True
    )
    summed = lax.psum_scatter(clip_share, "ctx", scatter_dimension=0, tiled=True).astype(
        jnp.float32
    )
    return (d_patches, summed)


LANES = 128
CELLS = GRID * GRID
WINDOW = WT * SW * SW
SIDES = GRID // SW
SPOTS = SIDES * SIDES
PAD = 16
FUSED_SLOTS = 640
NEG = -1e30
F32 = jnp.float32
BF16 = jnp.bfloat16


def mm(left, right):
    return lax.dot_general(left, right, (((1,), (0,)), ((), ())), preferred_element_type=F32)


def mm_nt(left, right):
    return lax.dot_general(left, right, (((1,), (1,)), ((), ())), preferred_element_type=F32)


def mm_tn(left, right):
    return lax.dot_general(left, right, (((0,), (0,)), ((), ())), preferred_element_type=F32)


def normed_rows(values):
    center = values - jnp.mean(values, axis=-1, keepdims=True)
    scale = lax.rsqrt(jnp.mean(center * center, axis=-1, keepdims=True) + norm_eps)
    return center * scale, scale


def norm_back(d_normed, unit, scale, gain):
    d_unit = d_normed * gain
    return scale * (
        d_unit
        - jnp.mean(d_unit, axis=-1, keepdims=True)
        - unit * jnp.mean(d_unit * unit, axis=-1, keepdims=True)
    )


def lane_mask(head, rows, lanes):
    lane = lax.broadcasted_iota(jnp.int32, (rows, lanes), 1)
    return (lane >= head * HEAD) & (lane < (head + 1) * HEAD)


def pack_kernel(shifts, patches, slots, cot, x_out, c_out):
    rows = cot.shape[0]
    count = patches.shape[0]
    tok = lax.broadcasted_iota(jnp.int32, (rows, LANES), 0)
    lane = lax.broadcasted_iota(jnp.int32, (rows, LANES), 1)
    tok_f = tok.astype(F32)
    step = jnp.floor((tok_f + 0.5) * (1.0 / CELLS))
    cell = tok_f - step * CELLS
    row = jnp.floor((cell + 0.5) * (1.0 / GRID))
    col = cell - row * GRID
    step_at, row_at, col_at = (shifts[0, axis].astype(F32) for axis in range(3))
    row = row - row_at
    row = jnp.where(row < 0, row + GRID, row)
    col = col - col_at
    col = jnp.where(col < 0, col + GRID, col)
    code = jnp.where(row >= SW, float(SIDES), 0.0) + jnp.where(col >= SW, 1.0, 0.0)
    code = code + jnp.where(step >= step_at, float(SPOTS), 0.0)
    hits = (lax.broadcasted_iota(jnp.int32, (rows, count), 0) == slots[...]).astype(F32)
    covered = jnp.sum(hits, axis=1, keepdims=True)
    hits = hits.astype(BF16)
    masked = jnp.where((lane.astype(F32) == code) & (covered < 0.5), 1.0, 0.0).astype(BF16)
    about = jnp.where(lane == 0, 1.0, jnp.where(lane == 1, code, 0.0)).astype(BF16)
    x_out[:, : patches.shape[1]] = patches[...]
    x_out[:, patches.shape[1] :] = mm_tn(hits, about).astype(BF16)
    c_out[:count, :] = mm_tn(hits, cot[...]).astype(BF16)
    sums = mm_tn(masked, cot[...])[: 2 * SPOTS]
    high = sums.astype(BF16).astype(F32)
    c_out[count:, :] = jnp.concatenate([high, sums - high], 0).astype(BF16)


def flat_rows(widths):
    places, at = [], 0
    for rows, lanes in widths:
        places.append(at)
        at += rows * lanes // LANES
    return places, at


def clip_kernel(n_dp, n_ctx, piece_rows, *refs):
    where_at = refs[0]
    x_blocks = refs[1 : 1 + n_ctx]
    c_blocks = refs[1 + n_ctx : 1 + 2 * n_ctx]
    (
        enc_gain,
        enc_qkv,
        enc_out,
        enc_to_dec,
        mask_token,
        dec_gain,
        dec_qkv,
        dec_out,
    ) = refs[1 + 2 * n_ctx : 9 + 2 * n_ctx]
    outs = refs[9 + 2 * n_ctx :]
    d_patches = outs[0]
    pieces = outs[1 : 1 + n_dp]
    (
        nrm,
        qkv,
        weights,
        mixed_sum,
        mixed,
        res,
        dec_in,
        dec_proj,
        meta,
        cots,
        sums,
        d_mixes,
        d_acc,
        blk_mix,
        blk_cot,
        d_res,
        d_mixed,
        d_scores,
        d_group,
        d_qkv,
        flat,
        cut,
    ) = outs[1 + n_dp :]
    core, dp_at, ctx_at = where_at[0], where_at[1], where_at[2]
    count = x_blocks[0].shape[0]
    slots = n_ctx * count
    width = enc_gain.shape[1]
    chans = enc_out.shape[0]
    dec_width = dec_gain.shape[1]
    dec_chans = dec_out.shape[0]
    group_lanes = 4 * HEAD
    groups = chans // group_lanes
    scale = HEAD ** (-0.5)
    half = n_ctx // 2

    def place(shard):
        shard = shard % n_ctx
        if shard % 2 == 0:
            return shard // 2
        at = shard // 2
        return jnp.where(core == 1, half + (at + 1) % half, half + at)

    for at in range(n_ctx):
        unit, _ = normed_rows(x_blocks[at][:, :width].astype(F32))
        nrm[at * count : (at + 1) * count, :] = (unit * enc_gain[...]).astype(BF16)
        meta[at * count : (at + 1) * count, :] = x_blocks[at][:, width:].astype(F32)
        cots[at * count : (at + 1) * count, :] = c_blocks[at][:count, :]
        high = c_blocks[at][count : count + 2 * SPOTS, :].astype(F32)
        low = c_blocks[at][count + 2 * SPOTS :, :].astype(F32)
        sums[at * 2 * SPOTS : (at + 1) * 2 * SPOTS, :] = high + low
    for at in range(3 * groups):
        lanes = slice(at * group_lanes, (at + 1) * group_lanes)
        qkv[:, lanes] = mm(nrm[...], enc_qkv[:, lanes]).astype(BF16)

    lane_of = lax.broadcasted_iota(jnp.int32, (8, LANES), 1)
    pick = jnp.where(lane_of == 0, 1.0, 0.0).astype(BF16)
    live_row = mm_nt(pick, meta[...].astype(BF16))[:1]
    bias = jnp.where(live_row > 0.5, 0.0, NEG)
    chunk = 2 * count
    chunks = slots // chunk

    def attend_group(group, carry):
        lanes = pl.ds(pl.multiple_of(group * group_lanes, group_lanes), group_lanes)
        key_lanes = pl.ds(pl.multiple_of(chans + group * group_lanes, group_lanes), group_lanes)
        value_lanes = pl.ds(
            pl.multiple_of(2 * chans + group * group_lanes, group_lanes), group_lanes
        )
        keys = qkv[:, key_lanes]
        values = qkv[:, value_lanes]
        for head in range(4):
            own = lane_mask(head, chunk, group_lanes)
            for part in range(chunks):
                rows = slice(part * chunk, (part + 1) * chunk)
                query = jnp.where(own, qkv[rows, lanes].astype(F32) * scale, 0.0).astype(BF16)
                scores = mm_nt(query, keys) + bias
                raised = jnp.exp(scores - jnp.max(scores, axis=-1, keepdims=True))
                share = (raised / jnp.sum(raised, axis=-1, keepdims=True)).astype(BF16)
                weights[group * 4 + head, rows, :] = share
                mix = mm(share, values)
                if head == 0:
                    mixed_sum[rows, :] = jnp.where(own, mix, 0.0)
                else:
                    mixed_sum[rows, :] = jnp.where(own, mix, mixed_sum[rows, :])
        mixed[:, lanes] = mixed_sum[...].astype(BF16)
        return carry

    lax.fori_loop(0, groups, attend_group, 0)

    for at in range(n_ctx):
        rows = slice(at * count, (at + 1) * count)
        out = x_blocks[at][:, :width].astype(F32) + mm(mixed[rows, :], enc_out[...])
        res[rows, :] = out.astype(BF16)
    dec_in[:slots, :] = mm(res[...], enc_to_dec[...]).astype(BF16)
    dec_in[slots:, :] = jnp.broadcast_to(mask_token[...], (PAD, dec_width)).astype(BF16)
    dec_unit, dec_scale = normed_rows(dec_in[...].astype(F32))
    dec_nrm = (dec_unit * dec_gain[...]).astype(BF16)
    dec_proj[...] = mm(dec_nrm, dec_qkv[...]).astype(BF16)
    d_mixes[...] = mm_nt(cots[...], dec_out[...]).astype(BF16)

    d_acc[...] = jnp.zeros_like(d_acc)
    size = 2 * count + PAD
    lane = lax.broadcasted_iota(jnp.int32, (count, LANES), 1).astype(F32)
    pad_row = lax.broadcasted_iota(jnp.int32, (PAD, LANES), 0)
    pad_lane = lax.broadcasted_iota(jnp.int32, (PAD, LANES), 1)
    eye = jnp.where((pad_row == pad_lane) & (pad_lane < SPOTS), 1.0, 0.0)
    col = lax.broadcasted_iota(jnp.int32, (size, size), 1)
    owns = [lane_mask(head, size, dec_chans) for head in range(dec_chans // HEAD)]
    heads = range(len(owns))

    def stack_heads(rows):
        return jnp.concatenate([jnp.where(own, rows, jnp.zeros_like(rows)) for own in owns], 0)

    def unstack_heads(rows):
        total = jnp.where(owns[0], rows[:size], 0.0)
        for head in heads[1:]:
            total = jnp.where(owns[head], rows[head * size : (head + 1) * size], total)
        return total

    for window in range(n_ctx):
        first, second = place(window), place(window + 1)
        rows_a = pl.ds(pl.multiple_of(first * count, PAD), count)
        rows_b = pl.ds(pl.multiple_of(second * count, PAD), count)

        def gathered(ref, last):
            return jnp.concatenate([ref[rows_a, :], ref[rows_b, :], last], 0)

        meta_a, meta_b = meta[rows_a, :], meta[rows_b, :]
        spot_a = meta_a[:, 1:2] - float(SPOTS)
        spot_b = meta_b[:, 1:2]
        hot_a = jnp.where((lane == spot_a) & (lane < SPOTS) & (meta_a[:, :1] > 0.5), 1.0, 0.0)
        hot_b = jnp.where((lane == spot_b) & (lane < SPOTS) & (meta_b[:, :1] > 0.5), 1.0, 0.0)
        hot_keys = jnp.concatenate([hot_a, hot_b, jnp.zeros_like(eye)], 0)
        hot_queries = jnp.concatenate([hot_a, hot_b, eye], 0)
        match = mm_nt(hot_queries.astype(BF16), hot_keys.astype(BF16))
        masked = float(WINDOW) - jnp.sum(match, axis=1, keepdims=True)
        mask_bias = jnp.where(masked > 0.5, jnp.log(jnp.maximum(masked, 1.0)), NEG)
        block_bias = jnp.where(
            match > 0.5, 0.0, jnp.where(col == 2 * count, mask_bias, NEG)
        )
        member = jnp.sum(hot_queries, axis=1, keepdims=True)
        rows_sum = jnp.concatenate(
            [
                sums[pl.ds(pl.multiple_of(first * 2 * SPOTS, 2 * SPOTS), 2 * SPOTS), :][SPOTS:]
                + sums[pl.ds(pl.multiple_of(second * 2 * SPOTS, 2 * SPOTS), 2 * SPOTS), :][:SPOTS],
                jnp.zeros((PAD - SPOTS, dec_width), F32),
            ],
            0,
        ).astype(BF16)
        block_cot = jnp.where(member > 0.5, gathered(cots, rows_sum).astype(F32), 0.0).astype(BF16)
        block_d_mix = mm_nt(rows_sum, dec_out[...]).astype(BF16)
        block_d_mix = jnp.where(
            member > 0.5, gathered(d_mixes, block_d_mix).astype(F32), 0.0
        )
        block = gathered(dec_proj, dec_proj[slots:, :])
        queries = stack_heads(block[:, :dec_chans].astype(F32) * scale).astype(BF16)
        keys = block[:, dec_chans : 2 * dec_chans]
        values = block[:, 2 * dec_chans :]
        scores = mm_nt(queries, keys) + jnp.concatenate([block_bias] * len(owns), 0)
        raised = jnp.exp(scores - jnp.max(scores, axis=-1, keepdims=True))
        share = raised / jnp.sum(raised, axis=-1, keepdims=True)
        share_low = share.astype(BF16)
        blk_mix[window * size : (window + 1) * size, :] = unstack_heads(
            mm(share_low, values)
        ).astype(BF16)
        blk_cot[window * size : (window + 1) * size, :] = block_cot
        d_stack = stack_heads(block_d_mix).astype(BF16)
        d_share = mm_nt(d_stack, values)
        delta = jnp.sum(d_share * share, axis=-1, keepdims=True)
        d_score = (share * (d_share - delta)).astype(BF16)
        d_query = unstack_heads(mm(d_score, keys)) * scale
        d_key = mm_tn(d_score, queries)
        d_value = mm_tn(share_low, d_stack)
        d_block = jnp.concatenate([d_query, d_key, d_value], 1)
        d_acc[rows_a, :] += d_block[:count]
        d_acc[rows_b, :] += d_block[count : 2 * count]
        mask_d_query = jnp.sum(d_block[2 * count : 2 * count + SPOTS, :dec_chans], 0, keepdims=True)
        d_acc[slots : slots + 1, :] += jnp.concatenate(
            [mask_d_query, d_block[2 * count : 2 * count + 1, dec_chans:]], 1
        )

    d_dec_proj = d_acc[...].astype(BF16)
    d_dec_nrm = mm_nt(d_dec_proj, dec_qkv[...])
    g_dec_qkv = mm_tn(dec_nrm, d_dec_proj)
    g_dec_out = mm_tn(blk_mix[...], blk_cot[...])
    g_dec_gain = jnp.sum(d_dec_nrm * dec_unit, axis=0, keepdims=True)
    d_dec_in = norm_back(d_dec_nrm, dec_unit, dec_scale, dec_gain[...])
    g_mask = jnp.sum(sums[...], axis=0, keepdims=True) + d_dec_in[slots : slots + 1]
    d_latent = (cots[...].astype(F32) + d_dec_in[:slots].astype(BF16).astype(F32)).astype(BF16)

    d_res[...] = mm_nt(d_latent, enc_to_dec[...]).astype(BF16)
    d_mixed[...] = mm_nt(d_res[...], enc_out[...]).astype(BF16)

    widths = [
        (1, width),
        enc_qkv.shape,
        enc_out.shape,
        enc_to_dec.shape,
        (1, dec_width),
        (1, dec_width),
        dec_qkv.shape,
        dec_out.shape,
    ]
    places, _ = flat_rows(widths)

    def store(which, lane_at, grad):
        stride = widths[which][1] // LANES
        for at in range(grad.shape[1] // LANES):
            tile = grad[:, at * LANES : (at + 1) * LANES]
            start = places[which] + lane_at // LANES + at
            if grad.shape[0] == 1:
                flat[start : start + 1, :] = tile
            else:
                flat[pl.ds(start, grad.shape[0], stride=stride), :] = tile

    store(2, 0, mm_tn(mixed[...], d_res[...]))
    store(3, 0, mm_tn(res[...], d_latent))
    store(4, 0, g_mask)
    store(5, 0, g_dec_gain)
    store(6, 0, g_dec_qkv)
    store(7, 0, g_dec_out)

    def attend_back(group, carry):
        lanes = pl.ds(pl.multiple_of(group * group_lanes, group_lanes), group_lanes)
        key_lanes = pl.ds(pl.multiple_of(chans + group * group_lanes, group_lanes), group_lanes)
        value_lanes = pl.ds(
            pl.multiple_of(2 * chans + group * group_lanes, group_lanes), group_lanes
        )
        keys = qkv[:, key_lanes]
        values = qkv[:, value_lanes]
        for head in range(4):
            own = lane_mask(head, chunk, group_lanes)
            every = lane_mask(head, slots, group_lanes)
            for part in range(chunks):
                rows = slice(part * chunk, (part + 1) * chunk)
                cot = jnp.where(own, d_mixed[rows, lanes].astype(F32), 0.0)
                delta = jnp.sum(cot * mixed[rows, lanes].astype(F32), axis=-1, keepdims=True)
                d_share = mm_nt(cot.astype(BF16), values)
                d_score = weights[group * 4 + head, rows, :].astype(F32) * (d_share - delta)
                d_score = d_score.astype(BF16)
                d_scores[rows, :] = d_score
                d_query = mm(d_score, keys) * scale
                if head == 0:
                    d_group[rows, :group_lanes] = jnp.where(own, d_query, 0.0)
                else:
                    d_group[rows, :group_lanes] = jnp.where(
                        own, d_query, d_group[rows, :group_lanes]
                    )
            query = qkv[:, lanes]
            d_key = mm_tn(d_scores[...], query) * scale
            d_value = mm_tn(weights[group * 4 + head], d_mixed[:, lanes])
            for at, grad in ((1, d_key), (2, d_value)):
                to = slice(at * group_lanes, (at + 1) * group_lanes)
                if head == 0:
                    d_group[:, to] = jnp.where(every, grad, 0.0)
                else:
                    d_group[:, to] = jnp.where(every, grad, d_group[:, to])
        d_qkv[:, lanes] = d_group[:, :group_lanes].astype(BF16)
        d_qkv[:, key_lanes] = d_group[:, group_lanes : 2 * group_lanes].astype(BF16)
        d_qkv[:, value_lanes] = d_group[:, 2 * group_lanes :].astype(BF16)
        return carry

    lax.fori_loop(0, groups, attend_back, 0)

    gain_sum = jnp.zeros((width, LANES), F32)
    for at in range(3 * groups):
        lanes = slice(at * group_lanes, (at + 1) * group_lanes)
        grad = mm_tn(nrm[...], d_qkv[:, lanes])
        store(1, at * group_lanes, grad)
        weighed = grad * enc_qkv[:, lanes].astype(F32)
        for to in range(group_lanes // LANES):
            gain_sum += weighed[:, to * LANES : (to + 1) * LANES]
    store(0, 0, jnp.sum(gain_sum.T, axis=0, keepdims=True) / enc_gain[...])
    d_own = mm_nt(d_qkv[:count, :], enc_qkv[...])
    unit, unit_scale = normed_rows(x_blocks[0][:, :width].astype(F32))
    d_own = norm_back(d_own, unit, unit_scale, enc_gain[...]).astype(BF16).astype(F32)
    d_patches[...] = (d_res[:count, :].astype(F32) + d_own).astype(BF16)

    share_half_rows = 2 * flat_rows(widths)[1] // (n_dp * n_ctx)
    for to in range(n_dp):
        start = (to * n_ctx + ctx_at) * share_half_rows // 2
        slot = lax.rem(to - dp_at + n_dp, n_dp)
        shift = lax.rem(start, 8)
        base = start - shift
        for small in range(8):

            @pl.when(shift == small)
            def _():
                rows = flat[pl.ds(pl.multiple_of(base, 8), piece_rows + 8), :]
                cut[slot] = rows[small : small + piece_rows].astype(BF16)

    for at in range(n_dp):
        pieces[at][...] = cut[at]


def join_kernel(where_at, *refs):
    out = refs[-1]
    total = refs[0][...].astype(F32)
    for ref in refs[1:-1]:
        total = total + ref[...].astype(F32)
    rows = out.shape[0]
    odd = lax.rem(where_at[2], 2) == 1

    @pl.when(odd)
    def _():
        turned = pltpu.roll(total, LANES // 2, 1)
        lane = lax.broadcasted_iota(jnp.int32, (rows, LANES), 1)
        out[...] = jnp.where(lane < LANES // 2, turned, pltpu.roll(turned, rows - 1, 0))

    @pl.when(jnp.logical_not(odd))
    def _():
        out[...] = total


def fused_body(
    n_dp,
    n_ctx,
    patches,
    vis_index,
    shifts,
    enc_gain,
    enc_qkv,
    enc_out,
    enc_to_dec,
    mask_token,
    dec_gain,
    dec_qkv,
    dec_out,
    dec_cot,
):
    count, width = patches.shape[1:]
    dec_width = dec_cot.shape[2]
    dec_chans = dec_out.shape[0]
    chans = enc_out.shape[0]
    slots = n_ctx * count
    vmem = pl.BlockSpec(memory_space=pltpu.VMEM)
    smem = pl.BlockSpec(memory_space=pltpu.SMEM)
    x_pay, c_pay = pl.pallas_call(
        pack_kernel,
        out_shape=(
            jax.ShapeDtypeStruct((count, width + LANES), BF16),
            jax.ShapeDtypeStruct((count + 4 * SPOTS, dec_width), BF16),
        ),
        in_specs=[smem, vmem, vmem, vmem],
        out_specs=(vmem, vmem),
        name="pack",
    )(shifts, patches[0], vis_index, dec_cot[0])

    half = n_ctx // 2
    swap = [(at, at ^ 1) for at in range(n_ctx)]

    def gather(block):
        near = [block]
        for step in range(1, half):
            turn = [(at, ((at // 2 - step) % half) * 2 + at % 2) for at in range(n_ctx)]
            near.append(lax.ppermute(block, "ctx", turn))
        return near + [lax.ppermute(other, "ctx", swap) for other in near]

    x_blocks = gather(x_pay)
    c_blocks = gather(c_pay)
    dp_at, ctx_at = lax.axis_index("dp"), lax.axis_index("ctx")
    where_at = jnp.stack([ctx_at % 2, dp_at, ctx_at]).astype(jnp.int32)

    params = (enc_gain, enc_qkv, enc_out, enc_to_dec, mask_token, dec_gain, dec_qkv, dec_out)
    length = sum(param.size for param in params)
    share = length // (n_dp * n_ctx)
    piece_rows = -(-(share + LANES // 2) // LANES)
    piece_rows = -(-piece_rows // PAD) * PAD
    size = 2 * count + PAD
    scratch = [
        pltpu.VMEM((slots, width), BF16),
        pltpu.VMEM((slots, 3 * chans), BF16),
        pltpu.VMEM((chans // HEAD, slots, slots), BF16),
        pltpu.VMEM((slots, 4 * HEAD), F32),
        pltpu.VMEM((slots, chans), BF16),
        pltpu.VMEM((slots, width), BF16),
        pltpu.VMEM((slots + PAD, dec_width), BF16),
        pltpu.VMEM((slots + PAD, 3 * dec_chans), BF16),
        pltpu.VMEM((slots, LANES), F32),
        pltpu.VMEM((slots, dec_width), BF16),
        pltpu.VMEM((n_ctx * 2 * SPOTS, dec_width), F32),
        pltpu.VMEM((slots, dec_chans), BF16),
        pltpu.VMEM((slots + PAD, 3 * dec_chans), F32),
        pltpu.VMEM((n_ctx * size, dec_chans), BF16),
        pltpu.VMEM((n_ctx * size, dec_width), BF16),
        pltpu.VMEM((slots, width), BF16),
        pltpu.VMEM((slots, chans), BF16),
        pltpu.VMEM((slots, slots), BF16),
        pltpu.VMEM((slots, 12 * HEAD), F32),
        pltpu.VMEM((slots, 3 * chans), BF16),
        pltpu.VMEM((length // LANES + 2 * PAD, LANES), F32),
        pltpu.VMEM((n_dp, piece_rows, LANES), BF16),
    ]
    piece = jax.ShapeDtypeStruct((piece_rows, LANES), BF16)
    d_patches, *pieces = pl.pallas_call(
        functools.partial(clip_kernel, n_dp, n_ctx, piece_rows),
        out_shape=[jax.ShapeDtypeStruct((count, width), BF16)] + [piece] * n_dp,
        in_specs=[smem] + [vmem] * (2 * n_ctx + 8),
        out_specs=[vmem] * (1 + n_dp),
        scratch_shapes=scratch,
        compiler_params=pltpu.CompilerParams(vmem_limit_bytes=VMEM_BYTES),
        name="clip",
    )(
        where_at,
        *x_blocks,
        *c_blocks,
        enc_gain[None],
        enc_qkv,
        enc_out,
        enc_to_dec,
        mask_token[None],
        dec_gain[None],
        dec_qkv,
        dec_out,
    )
    got = [pieces[0]]
    for step in range(1, n_dp):
        got.append(
            lax.ppermute(pieces[step], "dp", [(at, (at + step) % n_dp) for at in range(n_dp)])
        )
    summed = pl.pallas_call(
        join_kernel,
        out_shape=jax.ShapeDtypeStruct((piece_rows, LANES), F32),
        in_specs=[smem] + [vmem] * n_dp,
        out_specs=vmem,
        name="join",
    )(where_at, *got)
    return d_patches[None], summed.reshape(-1)[:share]


VMEM_BYTES = 60 * 1024 * 1024


def body(n_dp, n_ctx, patches, vis_index, *rest):
    dec_cot = rest[-1]
    small = n_ctx * patches.shape[1] <= FUSED_SLOTS
    if small and n_ctx % 2 == 0 and dec_cot.shape[1] == WT * CELLS:
        return fused_body(n_dp, n_ctx, patches, vis_index, *rest)
    return plain_body(patches, vis_index, *rest)


def solution(mesh):
    in_specs = (
        P("dp", "ctx", None),
        P("dp", "ctx"),
        P("dp", None),
        P(),
        P(),
        P(),
        P(),
        P(),
        P(),
        P(),
        P(),
        P("dp", "ctx", None),
    )
    out_specs = (P("dp", "ctx", None), P(("dp", "ctx")))
    return jax.shard_map(functools.partial(body, mesh.shape["dp"], mesh.shape["ctx"]), mesh=mesh, in_specs=in_specs, out_specs=out_specs, check_vma=False)
```

```python
import functools

import jax
import jax.numpy as jnp
from jax import lax
from jax.experimental import pallas as pl
from jax.experimental.pallas import tpu as pltpu
from jax.sharding import PartitionSpec as P

HEAD = 64
WT = 4
GRID = 14
SW = 7


norm_eps = 1e-06


def extended(block, sides, width):
    for axis, dim in sides:
        count = lax.axis_size(axis)
        forward = [(i, i + 1) for i in range(count - 1)]
        forward.append((count - 1, 0))
        backward = [(target, source) for source, target in forward]
        low = lax.ppermute(
            lax.slice_in_dim(block, block.shape[dim] - width, None, axis=dim), axis, forward
        )
        high = lax.ppermute(lax.slice_in_dim(block, 0, width, axis=dim), axis, backward)
        block = jnp.concatenate([low, block, high], axis=dim)
    return block


def layer_norm(inputs, gain):
    values = inputs.astype(jnp.float32)
    center = values - jnp.mean(values, axis=-1, keepdims=True)
    spread = jnp.mean(center * center, axis=-1, keepdims=True)
    return (center * lax.rsqrt(spread + norm_eps) * gain).astype(jnp.bfloat16)


def softmax_rows(scores):
    highest = jnp.max(scores, axis=-1, keepdims=True)
    raised = jnp.exp(scores - highest)
    return (raised / jnp.sum(raised, axis=-1, keepdims=True)).astype(jnp.bfloat16)


def enc_project(inputs, gain, weight):
    normed = layer_norm(inputs, gain)
    joined = jnp.dot(normed, weight, preferred_element_type=jnp.float32).astype(jnp.bfloat16)
    channels = weight.shape[1] // 3
    return (joined[:, :channels], joined[:, channels : 2 * channels], joined[:, 2 * channels :])


def enc_attend(query, key_all, value_all, live_all):
    query_rows = query.shape[0]
    key_rows = key_all.shape[0]
    head_count = query.shape[1] // HEAD
    query_heads = query.reshape(query_rows, head_count, HEAD).transpose(1, 0, 2)
    key_heads = key_all.reshape(key_rows, head_count, HEAD).transpose(1, 0, 2)
    value_heads = value_all.reshape(key_rows, head_count, HEAD).transpose(1, 0, 2)
    scores = jnp.einsum(
        "hrd,hkd->hrk", query_heads, key_heads, preferred_element_type=jnp.float32
    ) * HEAD ** (-0.5)
    scores = jnp.where(live_all[None, None, :] > 0.5, scores, -1e30)
    weights = softmax_rows(scores)
    mixed = jnp.einsum("hrk,hkd->hrd", weights, value_heads, preferred_element_type=jnp.float32)
    return mixed.transpose(1, 0, 2).reshape(query_rows, -1).astype(jnp.bfloat16)


def enc_finish(inputs, mixed, out_weight, down_weight):
    residual = (
        inputs.astype(jnp.float32) + jnp.dot(mixed, out_weight, preferred_element_type=jnp.float32)
    ).astype(jnp.bfloat16)
    return jnp.dot(residual, down_weight, preferred_element_type=jnp.float32).astype(jnp.bfloat16)


def build_grid(latent, slot_index, token, token_rows):
    base = jnp.broadcast_to(token, (token_rows, token.shape[0]))
    return base.at[slot_index].set(latent.astype(jnp.float32), mode="drop").astype(jnp.bfloat16)


def dec_project(dec_grid, gain, weight):
    normed = layer_norm(dec_grid, gain)
    joined = jnp.dot(normed, weight, preferred_element_type=jnp.float32).astype(jnp.bfloat16)
    channels = weight.shape[1] // 3
    return (joined[:, :channels], joined[:, channels:])


def dec_mix(query, pair_ext, dec_grid, offsets, weight):
    cell_count = GRID * GRID
    steps_own = query.shape[0] // cell_count
    channels = query.shape[1]
    window_span = steps_own + WT
    query_ext = jnp.pad(query.reshape(steps_own, cell_count, channels), ((WT, WT), (0, 0), (0, 0)))
    offset = (offsets[0] + WT - 1) % WT + 1 - WT
    slice_start = offset + WT
    query_win = lax.dynamic_slice_in_dim(query_ext, slice_start, window_span, 0)
    pair_win = lax.dynamic_slice_in_dim(pair_ext, slice_start, window_span, 0)
    joined = jnp.concatenate([query_win, pair_win], -1).reshape(
        window_span, GRID, GRID, 3 * channels
    )
    joined = jnp.roll(joined, (-offsets[1], -offsets[2]), axis=(1, 2))
    side_count = GRID // SW
    windows = joined.reshape(window_span // WT, WT, side_count, SW, side_count, SW, 3 * channels)
    windows = windows.transpose(0, 2, 4, 1, 3, 5, 6).reshape(-1, WT * SW * SW, 3 * channels)
    head_count = channels // HEAD
    window_count = windows.shape[0]
    token_count = windows.shape[1]
    query_heads = (
        windows[..., :channels]
        .reshape(window_count, token_count, head_count, HEAD)
        .transpose(0, 2, 1, 3)
    )
    key_heads = (
        windows[..., channels : 2 * channels]
        .reshape(window_count, token_count, head_count, HEAD)
        .transpose(0, 2, 1, 3)
    )
    value_heads = (
        windows[..., 2 * channels :]
        .reshape(window_count, token_count, head_count, HEAD)
        .transpose(0, 2, 1, 3)
    )
    scores = jnp.einsum(
        "nhqd,nhkd->nhqk", query_heads, key_heads, preferred_element_type=jnp.float32
    ) * HEAD ** (-0.5)
    weights = softmax_rows(scores)
    attended = jnp.einsum(
        "nhqk,nhkd->nhqd", weights, value_heads, preferred_element_type=jnp.float32
    ).astype(jnp.bfloat16)
    attended = attended.transpose(0, 2, 1, 3)
    attended = attended.reshape(window_span // WT, side_count, side_count, WT, SW, SW, channels)
    attended = attended.transpose(0, 3, 1, 4, 2, 5, 6).reshape(window_span, GRID, GRID, channels)
    attended = jnp.roll(attended, (offsets[1], offsets[2]), axis=(1, 2)).reshape(
        window_span, cell_count, channels
    )
    own_rows = lax.dynamic_slice_in_dim(attended, -offset, steps_own, 0).reshape(-1, channels)
    return dec_grid.astype(jnp.float32) + jnp.dot(
        own_rows, weight, preferred_element_type=jnp.float32
    )


def assemble(middle, from_left, from_right):
    total = middle.astype(jnp.float32)
    total = total + from_left.astype(jnp.float32)
    total = total + from_right.astype(jnp.float32)
    return total.astype(jnp.bfloat16)


def flatten(members):
    joined = jnp.concatenate([member.astype(jnp.float32).reshape(-1) for member in members])
    return joined


def plain_body(
    patches,
    vis_index,
    shifts,
    enc_gain,
    enc_qkv,
    enc_out,
    enc_to_dec,
    mask_token,
    dec_gain,
    dec_qkv,
    dec_out,
    dec_cot,
):
    tokens = patches[0]
    slot_index = vis_index[0]
    offsets = shifts[0]
    token_rows = dec_cot.shape[1]
    cell_count = GRID * GRID
    steps_own = token_rows // cell_count
    live_own = (slot_index < token_rows).astype(jnp.bfloat16)
    (query, key_own, value_own), project_pull = jax.vjp(enc_project, tokens, enc_gain, enc_qkv)
    key_all, value_all, live_all = (
        lax.all_gather(key_own, "ctx", axis=0, tiled=True),
        lax.all_gather(value_own, "ctx", axis=0, tiled=True),
        lax.all_gather(live_own, "ctx", axis=0, tiled=True),
    )

    def attend_fn(first, second, third):
        return enc_attend(first, second, third, live_all)

    mixed, attend_pull = jax.vjp(attend_fn, query, key_all, value_all)
    latent, finish_pull = jax.vjp(enc_finish, tokens, mixed, enc_out, enc_to_dec)

    def grid_fn(first, second):
        return build_grid(first, slot_index, second, token_rows)

    dec_grid, grid_pull = jax.vjp(grid_fn, latent, mask_token)
    (dec_query, dec_pair), dproj_pull = jax.vjp(dec_project, dec_grid, dec_gain, dec_qkv)
    pair_cube = dec_pair.reshape(steps_own, cell_count, dec_pair.shape[1])
    pair_ext = extended(pair_cube, (("ctx", 0),), WT)

    def mix_fn(first, second, third, fourth):
        return dec_mix(first, second, third, offsets, fourth)

    decoded, mix_pull = jax.vjp(mix_fn, dec_query, pair_ext, dec_grid, dec_out)
    d_query, d_ext, d_grid_mix, d_dout = mix_pull(dec_cot[0].astype(jnp.float32))
    rim_grads = jnp.concatenate([d_ext[:WT], d_ext[steps_own + WT :]], 0)
    beside_all = extended(rim_grads, (("ctx", 0),), WT)
    from_left = beside_all[:WT]
    from_right = beside_all[3 * WT :]
    d_pair = assemble(d_ext[WT : steps_own + WT], from_left, from_right).reshape(token_rows, -1)
    d_grid_proj, d_dgain, d_dqkv = dproj_pull((d_query, d_pair))
    d_grid = (d_grid_mix.astype(jnp.float32) + d_grid_proj.astype(jnp.float32)).astype(jnp.bfloat16)
    d_latent, d_mask = grid_pull(d_grid)
    d_tokens_res, d_mixed, d_eout, d_e2d = finish_pull(d_latent)
    d_query_enc, d_key_all, d_value_all = attend_pull(d_mixed)
    d_key, d_value = (
        lax.psum_scatter(
            d_key_all.astype(jnp.float32).astype(jnp.bfloat16),
            "ctx",
            scatter_dimension=0,
            tiled=True,
        ).astype(jnp.float32),
        lax.psum_scatter(
            d_value_all.astype(jnp.float32).astype(jnp.bfloat16),
            "ctx",
            scatter_dimension=0,
            tiled=True,
        ).astype(jnp.float32),
    )
    d_tokens_proj, d_egain, d_eqkv = project_pull(
        (d_query_enc, d_key.astype(jnp.bfloat16), d_value.astype(jnp.bfloat16))
    )
    d_patches = (d_tokens_res.astype(jnp.float32) + d_tokens_proj.astype(jnp.float32)).astype(
        jnp.bfloat16
    )[None]
    flat_grads = flatten((d_egain, d_eqkv, d_eout, d_e2d, d_mask, d_dgain, d_dqkv, d_dout))
    clip_share = lax.psum_scatter(
        flat_grads.astype(jnp.bfloat16), "dp", scatter_dimension=0, tiled=True
    )
    summed = lax.psum_scatter(clip_share, "ctx", scatter_dimension=0, tiled=True).astype(
        jnp.float32
    )
    return (d_patches, summed)


LANES = 128
CELLS = GRID * GRID
WINDOW = WT * SW * SW
SIDES = GRID // SW
SPOTS = SIDES * SIDES
PAD = 16
FUSED_SLOTS = 640
NEG = -1e30
F32 = jnp.float32
BF16 = jnp.bfloat16


def mm(left, right):
    return lax.dot_general(left, right, (((1,), (0,)), ((), ())), preferred_element_type=F32)


def mm_nt(left, right):
    return lax.dot_general(left, right, (((1,), (1,)), ((), ())), preferred_element_type=F32)


def mm_tn(left, right):
    return lax.dot_general(left, right, (((0,), (0,)), ((), ())), preferred_element_type=F32)


def normed_rows(values):
    center = values - jnp.mean(values, axis=-1, keepdims=True)
    scale = lax.rsqrt(jnp.mean(center * center, axis=-1, keepdims=True) + norm_eps)
    return center * scale, scale


def norm_back(d_normed, unit, scale, gain):
    d_unit = d_normed * gain
    return scale * (
        d_unit
        - jnp.mean(d_unit, axis=-1, keepdims=True)
        - unit * jnp.mean(d_unit * unit, axis=-1, keepdims=True)
    )


def lane_mask(head, rows, lanes):
    lane = lax.broadcasted_iota(jnp.int32, (rows, lanes), 1)
    return (lane >= head * HEAD) & (lane < (head + 1) * HEAD)


def pack_kernel(shifts, tokens, slots, cot, out):
    rows, width = cot.shape
    front = tokens.shape[1]
    count = slots.shape[1]
    tok = lax.broadcasted_iota(jnp.int32, (rows, LANES), 0)
    lane = lax.broadcasted_iota(jnp.int32, (rows, LANES), 1)
    tok_f = tok.astype(F32)
    step = jnp.floor((tok_f + 0.5) * (1.0 / CELLS))
    cell = tok_f - step * CELLS
    row = jnp.floor((cell + 0.5) * (1.0 / GRID))
    col = cell - row * GRID
    step_at, row_at, col_at = (shifts[0, axis].astype(F32) for axis in range(3))
    row = row - row_at
    row = jnp.where(row < 0, row + GRID, row)
    col = col - col_at
    col = jnp.where(col < 0, col + GRID, col)
    code = jnp.where(row >= SW, float(SIDES), 0.0) + jnp.where(col >= SW, 1.0, 0.0)
    code = code + jnp.where(step >= step_at, float(SPOTS), 0.0)
    hits = (lax.broadcasted_iota(jnp.int32, (rows, count), 0) == slots[...]).astype(F32)
    covered = jnp.sum(hits, axis=1, keepdims=True)
    hits = hits.astype(BF16)
    masked = jnp.where((lane.astype(F32) == code) & (covered < 0.5), 1.0, 0.0).astype(BF16)
    about = jnp.where(lane == 0, code + 1.0, 0.0).astype(BF16)
    out[:, :front] = tokens[...]
    out[:, front : front + width] = mm_tn(hits, cot[...]).astype(BF16)
    sums = mm_tn(masked, cot[...])[: 2 * SPOTS]
    codes = mm_tn(about, hits)[:8]
    codes = jnp.concatenate([codes, jnp.zeros((8, LANES - count), F32)], 1)
    rest = [sums[:, at * LANES : (at + 1) * LANES] for at in range(width // LANES)] + [codes]
    spare = count - 8 * len(rest)
    rest = jnp.concatenate(rest + [jnp.zeros((spare, LANES), F32)], 0)
    out[:, front + width :] = rest.astype(BF16)


def flat_rows(widths):
    places, at = [], 0
    for rows, lanes in widths:
        places.append(at)
        at += rows * lanes // LANES
    return places, at


def store_flat(flat, widths, offset, which, lane_at, grad):
    places, _ = flat_rows(widths)
    stride = widths[which][1] // LANES
    for at in range(grad.shape[1] // LANES):
        tile = grad[:, at * LANES : (at + 1) * LANES]
        start = places[which] - offset + lane_at // LANES + at
        if grad.shape[0] == 1:
            flat[start : start + 1, :] = tile
        else:
            flat[pl.ds(start, grad.shape[0], stride=stride), :] = tile


def head_lanes(head, rows, lanes):
    lane = lax.broadcasted_iota(jnp.int32, (rows, lanes), 1)
    return (lane >= head * HEAD) & (lane < (head + 1) * HEAD)


def clip_kernel(n_dp, n_ctx, n_blocks, widths, *refs):
    where_at = refs[0]
    blocks = refs[1 : 1 + n_blocks]
    enc_gain, mask_token, dec_gain = refs[1 + n_blocks : 4 + n_blocks]
    far = refs[4 + n_blocks : 9 + n_blocks]
    outs = refs[9 + n_blocks :]
    d_patches = outs[0]
    pieces = outs[1 : 1 + n_dp]
    (
        nrm,
        nrm_t,
        qkv,
        weights,
        mixed,
        res,
        dec_in,
        dec_proj,
        hot,
        sums,
        d_mixes,
        d_acc,
        blk_mix,
        blk_cot,
        wide,
        q_stack,
        d_stack,
        p_stack,
        d_p_stack,
        d_query,
        d_keys,
        d_values,
        d_latent,
        d_mixed,
        turned,
        d_scores,
        d_kv_t,
        d_qkv,
        bias,
        enc_qkv_here,
        enc_out_here,
        enc_to_dec_here,
        dec_qkv_here,
        dec_out_here,
        flat,
        cut,
        sems,
    ) = outs[1 + n_dp :]
    here = (enc_qkv_here, enc_out_here, enc_to_dec_here, dec_qkv_here, dec_out_here)
    loads = [
        pltpu.make_async_copy(far[at], here[at], sems.at[at]) for at in range(len(here))
    ]
    loads[0].start()
    core = where_at[0]
    count, width = blocks[0].shape[0], enc_gain.shape[1]
    slots = n_ctx * count
    chans = enc_out_here.shape[0]
    dec_chans, dec_width = dec_out_here.shape
    group_lanes = 4 * HEAD
    groups = chans // group_lanes
    scale = HEAD ** (-0.5)
    half = n_ctx // 2
    spread = 2 * SPOTS
    size = count + PAD
    chunk = slots // 2

    tokens_at = slice(0, width)
    cots_at = slice(width, width + dec_width)
    rest_at = slice(width + dec_width, width + dec_width + LANES)

    def pick(at, lanes):
        chip = where_at[2] // 2
        block = blocks[at][:, lanes]
        hop = at % half
        if n_blocks == n_ctx or hop not in (1, half - 1):
            return block
        other = blocks[n_ctx + at // half][:, lanes]
        return jnp.where(chip == (half - 1 if hop == 1 else 0), other, block)

    def codes_of(rest):
        at = spread * dec_width // LANES
        return rest[at : at + 8, :count]

    for at in range(n_ctx):
        rows = slice(at * count, (at + 1) * count)
        unit, _ = normed_rows(pick(at, tokens_at).astype(F32))
        nrm[rows, :] = (unit * enc_gain[...]).astype(BF16)
        codes = codes_of(pick(at, rest_at).astype(F32))[:1]
        bias[:, rows] = jnp.broadcast_to(jnp.where(codes > 0.5, 0.0, NEG), (8, count))
    for load in loads[1:]:
        load.start()
    loads[0].wait()

    for at in range(3 * groups):
        lanes = slice(at * group_lanes, (at + 1) * group_lanes)
        qkv[:, lanes] = mm(nrm[...], enc_qkv_here[:, lanes]).astype(BF16)
    nrm_t[...] = nrm[...].T

    def lanes_of(group):
        return [
            pl.ds(pl.multiple_of(at * chans + group * group_lanes, group_lanes), group_lanes)
            for at in range(3)
        ]

    def attend(group, carry):
        lanes, key_lanes, value_lanes = lanes_of(group)
        keys = qkv[:, key_lanes]
        values = qkv[:, value_lanes]
        for head in range(4):
            own = head_lanes(head, chunk, group_lanes)
            for part in range(slots // chunk):
                rows = slice(part * chunk, (part + 1) * chunk)
                query = jnp.where(own, qkv[rows, lanes].astype(F32) * scale, 0.0).astype(BF16)
                scores = mm_nt(query, keys) + bias[:1]
                raised = jnp.exp(scores - jnp.max(scores, axis=-1, keepdims=True))
                share = (raised * (1.0 / jnp.sum(raised, axis=-1, keepdims=True))).astype(BF16)
                weights[group * 4 + head, rows, :] = share
                mix = mm(share, values)
                if head > 0:
                    mix = jnp.where(own, mix, mixed[rows, lanes].astype(F32))
                mixed[rows, lanes] = mix.astype(BF16)
        return carry

    lax.fori_loop(0, groups, attend, 0)

    loads[1].wait()
    loads[2].wait()
    for at in range(n_ctx):
        rows = slice(at * count, (at + 1) * count)
        out = pick(at, tokens_at).astype(F32) + mm(mixed[rows, :], enc_out_here[...])
        res[rows, :] = out.astype(BF16)
    latent = mm(res[...], enc_to_dec_here[...]).astype(BF16)
    d_latent[...] = latent

    def place(shard, on_core):
        at = shard // 2
        if shard % 2 == 0:
            return at
        return half + (at + on_core) % half

    def rows_of(shard):
        shard = shard % n_ctx
        return slice(shard * count, (shard + 1) * count)

    lane = lax.broadcasted_iota(jnp.int32, (count, LANES), 1).astype(F32)
    square = [lax.broadcasted_iota(jnp.int32, (count, count), axis) for axis in range(2)]
    unity = jnp.where(square[0] == square[1], 1.0, 0.0).astype(BF16)

    def in_time(shard, at):
        dec_in[rows_of(shard), :] = d_latent[rows_of(at), :]
        blk_cot[shard * size : shard * size + count, :] = pick(at, cots_at)
        rest = pick(at, rest_at).astype(F32)
        sums[shard * spread : (shard + 1) * spread, :] = jnp.concatenate(
            [rest[tile * spread : (tile + 1) * spread] for tile in range(dec_width // LANES)], 1
        )
        code = mm_nt(unity, codes_of(rest).astype(BF16))[:, :1] - 1.0
        last = (shard + n_ctx - 1) % n_ctx
        window = code + jnp.where(
            code >= SPOTS, float((shard - 1) * SPOTS), float(last * SPOTS)
        )
        hit = (lane == window) & (code >= 0.0)
        hot[rows_of(shard), :] = jnp.where(hit, 1.0, 0.0).astype(BF16)

    for shard in range(0, n_ctx, 2):
        in_time(shard, place(shard, 0))
    for on_core in range(2):

        @pl.when(core == on_core)
        def _():
            for shard in range(1, n_ctx, 2):
                in_time(shard, place(shard, on_core))

    loads[3].wait()
    loads[4].wait()
    dec_in[slots:, :] = jnp.broadcast_to(mask_token[...], (PAD, dec_width)).astype(BF16)
    for shard in range(n_ctx):
        after = (shard + 1) % n_ctx
        rows_sum = (
            sums[shard * spread + SPOTS : (shard + 1) * spread, :]
            + sums[after * spread : after * spread + SPOTS, :]
        )
        blk_cot[shard * size + count : (shard + 1) * size, :] = jnp.concatenate(
            [rows_sum, jnp.zeros((PAD - SPOTS, dec_width), F32)], 0
        ).astype(BF16)

    dec_unit, dec_scale = normed_rows(dec_in[...].astype(F32))
    dec_nrm = (dec_unit * dec_gain[...]).astype(BF16)
    dec_proj[...] = mm(dec_nrm, dec_qkv_here[...]).astype(BF16)
    d_mixes[...] = mm_nt(blk_cot[...], dec_out_here[...]).astype(BF16)

    pad_row = lax.broadcasted_iota(jnp.int32, (PAD, LANES), 0)
    pad_lane = lax.broadcasted_iota(jnp.int32, (PAD, LANES), 1)
    reach = 3 * count + PAD
    col = lax.broadcasted_iota(jnp.int32, (size, reach), 1)
    owns = [head_lanes(head, size, dec_chans) for head in range(dec_chans // HEAD)]
    tall = len(owns) * size
    mask_rows = slice(slots, slots + PAD)
    query_lanes = slice(0, dec_chans)
    key_lanes = slice(dec_chans, 2 * dec_chans)
    value_lanes = slice(2 * dec_chans, 3 * dec_chans)

    def stack_heads(rows):
        return jnp.concatenate([jnp.where(own, rows, 0.0) for own in owns], 0)

    def unstack_heads(rows):
        total = jnp.where(owns[0], rows[:size], 0.0)
        for head in range(1, len(owns)):
            total = jnp.where(owns[head], rows[head * size : (head + 1) * size], total)
        return total

    def rows_at(shard, rows):
        return pl.ds(pl.multiple_of(shard * rows, PAD), rows)

    def near(ref, shard, lanes, last):
        shards = [lax.rem(shard + n_ctx + step, n_ctx) for step in (-1, 0, 1)]
        return jnp.concatenate([ref[rows_at(at, count), lanes] for at in shards] + [last], 0)

    def keys_of(shard):
        return near(dec_proj, shard, key_lanes, dec_proj[mask_rows, key_lanes])

    def values_of(shard):
        return near(dec_proj, shard, value_lanes, dec_proj[mask_rows, value_lanes])

    def score(shard, here):
        eye = (pad_row + shard * SPOTS == pad_lane) & (pad_row < SPOTS)
        eye = jnp.where(eye, 1.0, 0.0).astype(BF16)
        hot_keys = near(hot, shard, slice(None), jnp.zeros((PAD, LANES), BF16))
        match = mm_nt(jnp.concatenate([hot[rows_at(shard, count), :], eye], 0), hot_keys)
        masked = float(WINDOW) - jnp.sum(match, axis=1, keepdims=True)
        mask_bias = jnp.where(masked > 0.5, jnp.log(jnp.maximum(masked, 1.0)), NEG)
        block_bias = jnp.where(match > 0.5, 0.0, jnp.where(col == 3 * count, mask_bias, NEG))
        queries = jnp.concatenate(
            [dec_proj[rows_at(shard, count), query_lanes], dec_proj[mask_rows, query_lanes]], 0
        )
        queries = stack_heads(queries.astype(F32) * scale).astype(BF16)
        q_stack[here, :] = queries
        d_stack[here, :] = stack_heads(d_mixes[rows_at(shard, size), :].astype(F32)).astype(BF16)
        wide[here, :] = mm_nt(queries, keys_of(shard)) + jnp.concatenate(
            [block_bias] * len(owns), 0
        )

    def soften():
        scores = wide[...]
        raised = jnp.exp(scores - jnp.max(scores, axis=-1, keepdims=True))
        share = raised * (1.0 / jnp.sum(raised, axis=-1, keepdims=True))
        p_stack[...] = share.astype(BF16)

    def mix(shard, here):
        values = values_of(shard)
        blk_mix[rows_at(shard, size), :] = unstack_heads(mm(p_stack[here, :], values)).astype(BF16)
        wide[here, :] = mm_nt(d_stack[here, :], values)

    def soften_back():
        share = p_stack[...].astype(F32)
        d_share = wide[...]
        delta = jnp.sum(d_share * share, axis=-1, keepdims=True)
        d_p_stack[...] = (share * (d_share - delta)).astype(BF16)

    def mix_back(shard, here):
        d_score = d_p_stack[here, :]
        d_query[rows_at(shard, size), :] = unstack_heads(mm(d_score, keys_of(shard))) * scale
        d_keys[shard] = mm_tn(d_score, q_stack[here, :]).astype(BF16)
        d_values[shard] = mm_tn(p_stack[here, :], d_stack[here, :]).astype(BF16)

    def two_shards(at, carry):
        both = [(2 * at + one, slice(one * tall, (one + 1) * tall)) for one in range(2)]
        for shard, here in both:
            score(shard, here)
        soften()
        for shard, here in both:
            mix(shard, here)
        soften_back()
        for shard, here in both:
            mix_back(shard, here)
        return carry

    lax.fori_loop(0, half, two_shards, 0)

    mask_d_query = jnp.zeros((1, dec_chans), F32)
    mask_d_pair = [jnp.zeros((1, dec_chans), F32) for _ in range(2)]
    for shard in range(n_ctx):
        rows = rows_of(shard)
        d_acc[rows, query_lanes] = d_query[shard * size : shard * size + count, :].astype(BF16)
        mask_d_query += jnp.sum(
            d_query[shard * size + count : shard * size + count + SPOTS, :], 0, keepdims=True
        )
        for at, (lanes, ref) in enumerate(((key_lanes, d_keys), (value_lanes, d_values))):
            before, after = (shard + n_ctx - 1) % n_ctx, (shard + 1) % n_ctx
            total = (
                ref[before, 2 * count : 3 * count, :].astype(F32)
                + ref[shard, count : 2 * count, :].astype(F32)
                + ref[after, :count, :].astype(F32)
            )
            d_acc[rows, lanes] = total.astype(BF16)
            mask_d_pair[at] += ref[shard, 3 * count :, :].astype(F32)[:1]
    first = lax.broadcasted_iota(jnp.int32, (PAD, 3 * dec_chans), 0) == 0
    mask_d = jnp.concatenate([mask_d_query] + mask_d_pair, 1)
    d_acc[mask_rows, :] = jnp.where(first, mask_d, 0.0).astype(BF16)

    d_dec_proj = d_acc[...]
    d_dec_nrm = mm_nt(d_dec_proj, dec_qkv_here[...])
    g_dec_qkv = mm_tn(dec_nrm, d_dec_proj)
    g_dec_out = mm_tn(blk_mix[...], blk_cot[...])
    g_dec_gain = jnp.sum(d_dec_nrm * dec_unit, axis=0, keepdims=True)
    d_dec_in = norm_back(d_dec_nrm, dec_unit, dec_scale, dec_gain[...])
    g_mask = jnp.sum(sums[...], axis=0, keepdims=True) + d_dec_in[slots : slots + 1]
    for shard in range(n_ctx):
        cot = blk_cot[shard * size : shard * size + count, :].astype(F32)
        back = d_dec_in[shard * count : (shard + 1) * count].astype(BF16).astype(F32)
        dec_in[rows_of(shard), :] = (cot + back).astype(BF16)
    for on_core in range(2):

        @pl.when(core == on_core)
        def _():
            for shard in range(n_ctx):
                d_latent[rows_of(place(shard, on_core)), :] = dec_in[rows_of(shard), :]

    d_res = nrm
    d_res[...] = mm_nt(d_latent[...], enc_to_dec_here[...]).astype(BF16)
    d_mixed[...] = mm_nt(d_res[...], enc_out_here[...]).astype(BF16)

    def store(which, lane_at, grad):
        store_flat(flat, widths, 0, which, lane_at, grad)

    store(2, 0, mm_tn(mixed[...], d_res[...]))
    store(3, 0, mm_tn(res[...], d_latent[...]))
    store(4, 0, g_mask)
    store(5, 0, g_dec_gain)
    store(6, 0, g_dec_qkv)
    store(7, 0, g_dec_out)

    def attend_back(group, carry):
        lanes, key_lanes, value_lanes = lanes_of(group)
        turned[:group_lanes, :] = qkv[:, lanes].T
        turned[group_lanes:, :] = d_mixed[:, lanes].T
        keys = qkv[:, key_lanes]
        values = qkv[:, value_lanes]
        for head in range(4):
            own = head_lanes(head, chunk, group_lanes)
            at_head = group * 4 + head
            for part in range(slots // chunk):
                rows = slice(part * chunk, (part + 1) * chunk)
                cot = jnp.where(own, d_mixed[rows, lanes].astype(F32), 0.0)
                delta = jnp.sum(cot * mixed[rows, lanes].astype(F32), axis=-1, keepdims=True)
                d_share = mm_nt(cot.astype(BF16), values)
                d_score = weights[at_head, rows, :].astype(F32) * (d_share - delta)
                d_score = d_score.astype(BF16)
                d_scores[head % 2, rows, :] = d_score
                d_query = mm(d_score, keys) * scale
                if head > 0:
                    d_query = jnp.where(own, d_query, d_qkv[rows, lanes].astype(F32))
                d_qkv[rows, lanes] = d_query.astype(BF16)
            to_key = pl.ds(pl.multiple_of(at_head * HEAD, HEAD), HEAD)
            to_value = pl.ds(pl.multiple_of(chans + at_head * HEAD, HEAD), HEAD)
            query_t = turned[head * HEAD : (head + 1) * HEAD, :]
            cot_t = turned[group_lanes + head * HEAD : group_lanes + (head + 1) * HEAD, :]
            d_kv_t[to_key, :] = mm(query_t, d_scores[head % 2]) * scale
            d_kv_t[to_value, :] = mm(cot_t, weights[at_head])
        return carry

    lax.fori_loop(0, groups, attend_back, 0)
    d_qkv[:, chans:] = d_kv_t[...].T.astype(BF16)

    places, total = flat_rows(widths)
    gain_sum = jnp.zeros((width, LANES), F32)
    for at in range(3 * groups):
        lanes = slice(at * group_lanes, (at + 1) * group_lanes)
        grad = mm(nrm_t[...], d_qkv[:, lanes])
        store(1, at * group_lanes, grad)
        weighed = grad * enc_qkv_here[:, lanes].astype(F32)
        for to in range(group_lanes // LANES):
            gain_sum += weighed[:, to * LANES : (to + 1) * LANES]
    store(0, 0, jnp.sum(gain_sum.T, axis=0, keepdims=True) / enc_gain[...])
    d_own = mm_nt(d_qkv[:count, :], enc_qkv_here[...])
    unit, unit_scale = normed_rows(blocks[0][:, tokens_at].astype(F32))
    d_own = norm_back(d_own, unit, unit_scale, enc_gain[...]).astype(BF16).astype(F32)
    d_patches[...] = (d_res[:count, :].astype(F32) + d_own).astype(BF16)

    piece_rows = cut.shape[1]
    half_rows = 2 * total // (n_dp * n_ctx)

    def cut_piece(to, carry):
        start = (to * n_ctx + where_at[2]) * half_rows // 2
        slot = lax.rem(to - where_at[1] + n_dp, n_dp)
        shift = lax.rem(start, 8)
        base = start - shift
        for small in range(8):

            @pl.when(shift == small)
            def _():
                rows = flat[pl.ds(pl.multiple_of(base, 8), piece_rows + 8), :]
                cut[slot] = rows[small : small + piece_rows].astype(BF16)

        return carry

    lax.fori_loop(0, n_dp, cut_piece, 0)
    for at in range(n_dp):
        pieces[at][...] = cut[at]


def join_kernel(where_at, *refs):
    out = refs[-1]
    total = refs[0][...].astype(F32)
    for ref in refs[1:-1]:
        total = total + ref[...].astype(F32)
    rows = out.shape[0]
    odd = lax.rem(where_at[2], 2) == 1

    @pl.when(odd)
    def _():
        turned = pltpu.roll(total, LANES // 2, 1)
        lane = lax.broadcasted_iota(jnp.int32, (rows, LANES), 1)
        out[...] = jnp.where(lane < LANES // 2, turned, pltpu.roll(turned, rows - 1, 0))

    @pl.when(jnp.logical_not(odd))
    def _():
        out[...] = total


def fused_body(
    n_dp,
    n_ctx,
    patches,
    vis_index,
    shifts,
    enc_gain,
    enc_qkv,
    enc_out,
    enc_to_dec,
    mask_token,
    dec_gain,
    dec_qkv,
    dec_out,
    dec_cot,
):
    tokens = patches[0]
    params = (enc_gain, enc_qkv, enc_out, enc_to_dec, mask_token, dec_gain, dec_qkv, dec_out)
    widths = [(1,) * (2 - param.ndim) + param.shape for param in params]
    half = n_ctx // 2

    def by_hops(block):
        def shift(array, hops, chips):
            pairs = [((chip + hops) % half, chip) for chip in chips]
            turn = [(2 * pair[0] + core, 2 * pair[1] + core) for pair in pairs for core in range(2)]
            return lax.ppermute(array, "ctx", turn)

        def swap(array, chips):
            return lax.ppermute(
                array, "ctx", [(2 * chip + core, 2 * chip + 1 - core) for chip in chips for core in range(2)]
            )

        every = range(half)
        if half != 4:
            near = [block] + [shift(block, step, every) for step in range(1, half)]
            return near + [swap(other, every) for other in near]
        where = (every, every[:-1], every, every[1:], (0, half - 1))
        middle = shift(block, 2, every)
        first, last = shift(block, 1, where[1]), shift(block, 3, where[3])
        ends = lax.ppermute(
            middle, "ctx", [(2 * a + core, 2 * b + core) for a, b in ((1, 0), (2, 3)) for core in range(2)]
        )
        near = [block, first, middle, last, ends]
        far = [swap(other, chips) for other, chips in zip(near, where)]
        return near[:4] + far[:4] + [near[4], far[4]]

    blocks = by_hops(call_pack(shifts, tokens, vis_index, dec_cot[0]))
    dp_at, ctx_at = lax.axis_index("dp"), lax.axis_index("ctx")
    where_at = jnp.stack([ctx_at % 2, dp_at, ctx_at]).astype(jnp.int32)
    d_patches, *pieces = call_clip(n_dp, n_ctx, widths, where_at, blocks, params)
    got = [pieces[0]]
    for step in range(1, n_dp):
        turn = [(at, (at + step) % n_dp) for at in range(n_dp)]
        got.append(lax.ppermute(pieces[step], "dp", turn))
    share = flat_rows(widths)[1] * LANES // (n_dp * n_ctx)
    return d_patches[None], call_join(where_at, got).reshape(-1)[:share]


def piece_shape(n_dp, n_ctx, widths):
    share = flat_rows(widths)[1] * LANES // (n_dp * n_ctx)
    rows = -(-(share + LANES // 2) // LANES)
    return jax.ShapeDtypeStruct((-(-rows // PAD) * PAD, LANES), BF16)


IN_VMEM = pl.BlockSpec(memory_space=pltpu.VMEM)
IN_SMEM = pl.BlockSpec(memory_space=pltpu.SMEM)
ANYWHERE = pl.BlockSpec(memory_space=pl.ANY)


def call_pack(shifts, tokens, vis_index, cot):
    count, width = tokens.shape
    return pl.pallas_call(
        pack_kernel,
        out_shape=jax.ShapeDtypeStruct((count, width + cot.shape[1] + LANES), BF16),
        in_specs=[IN_SMEM, IN_VMEM, IN_VMEM, IN_VMEM],
        out_specs=IN_VMEM,
        name="pack",
    )(shifts, tokens, vis_index, cot)


def call_clip(n_dp, n_ctx, widths, where_at, blocks, params):
    enc_gain, enc_qkv, enc_out, enc_to_dec, mask_token, dec_gain, dec_qkv, dec_out = params
    count, width = blocks[0].shape[0], enc_gain.shape[0]
    slots = n_ctx * count
    chans = enc_out.shape[0]
    dec_chans, dec_width = dec_out.shape
    total = flat_rows(widths)[1]
    piece = piece_shape(n_dp, n_ctx, widths)
    size = count + PAD
    tall = dec_chans // HEAD * size
    reach = 3 * count + PAD
    matrices = (enc_qkv, enc_out, enc_to_dec, dec_qkv, dec_out)
    return pl.pallas_call(
        functools.partial(clip_kernel, n_dp, n_ctx, len(blocks), widths),
        out_shape=[jax.ShapeDtypeStruct((count, width), BF16)] + [piece] * n_dp,
        in_specs=[IN_SMEM] + [IN_VMEM] * (len(blocks) + 3) + [ANYWHERE] * len(matrices),
        out_specs=[IN_VMEM] * (1 + n_dp),
        scratch_shapes=[
            pltpu.VMEM((slots, width), BF16),
            pltpu.VMEM((width, slots), BF16),
            pltpu.VMEM((slots, 3 * chans), BF16),
            pltpu.VMEM((chans // HEAD, slots, slots), BF16),
            pltpu.VMEM((slots, chans), BF16),
            pltpu.VMEM((slots, width), BF16),
            pltpu.VMEM((slots + PAD, dec_width), BF16),
            pltpu.VMEM((slots + PAD, 3 * dec_chans), BF16),
            pltpu.VMEM((slots, LANES), BF16),
            pltpu.VMEM((n_ctx * 2 * SPOTS, dec_width), F32),
            pltpu.VMEM((n_ctx * size, dec_chans), BF16),
            pltpu.VMEM((slots + PAD, 3 * dec_chans), BF16),
            pltpu.VMEM((n_ctx * size, dec_chans), BF16),
            pltpu.VMEM((n_ctx * size, dec_width), BF16),
            pltpu.VMEM((2 * tall, reach), F32),
            pltpu.VMEM((2 * tall, dec_chans), BF16),
            pltpu.VMEM((2 * tall, dec_chans), BF16),
            pltpu.VMEM((2 * tall, reach), BF16),
            pltpu.VMEM((2 * tall, reach), BF16),
            pltpu.VMEM((n_ctx * size, dec_chans), F32),
            pltpu.VMEM((n_ctx, reach, dec_chans), BF16),
            pltpu.VMEM((n_ctx, reach, dec_chans), BF16),
            pltpu.VMEM((slots, dec_width), BF16),
            pltpu.VMEM((slots, chans), BF16),
            pltpu.VMEM((8 * HEAD, slots), BF16),
            pltpu.VMEM((2, slots, slots), BF16),
            pltpu.VMEM((2 * chans, slots), F32),
            pltpu.VMEM((slots, 3 * chans), BF16),
            pltpu.VMEM((8, slots), F32),
        ]
        + [pltpu.VMEM(matrix.shape, BF16) for matrix in matrices]
        + [
            pltpu.VMEM((total + 2 * PAD, LANES), F32),
            pltpu.VMEM((n_dp,) + piece.shape, BF16),
            pltpu.SemaphoreType.DMA((len(matrices),)),
        ],
        compiler_params=pltpu.CompilerParams(vmem_limit_bytes=VMEM_BYTES),
        cost_estimate=pl.CostEstimate(
            flops=40 * 10**9, bytes_accessed=16 * 2**20, transcendentals=0
        ),
        name="clip",
    )(
        where_at,
        *blocks,
        enc_gain[None],
        mask_token[None],
        dec_gain[None],
        *matrices,
    )


def call_join(where_at, blocks):
    return pl.pallas_call(
        join_kernel,
        out_shape=jax.ShapeDtypeStruct(blocks[0].shape, F32),
        in_specs=[IN_SMEM] + [IN_VMEM] * len(blocks),
        out_specs=IN_VMEM,
        name="join",
    )(where_at, *blocks)


VMEM_BYTES = 56 * 1024 * 1024


def body(n_dp, n_ctx, patches, vis_index, *rest):
    enc_qkv = rest[2]
    dec_cot = rest[-1]
    head = enc_qkv.shape[0] * (1 + enc_qkv.shape[1])
    length = sum(param.size for param in rest[1:-1])
    small = n_ctx * patches.shape[1] <= FUSED_SLOTS
    whole = head * n_dp % length == 0 and dec_cot.shape[1] == WT * CELLS
    if small and n_ctx % 2 == 0 and whole:
        return fused_body(n_dp, n_ctx, patches, vis_index, *rest)
    return plain_body(patches, vis_index, *rest)


def solution(mesh):
    in_specs = (
        P("dp", "ctx", None),
        P("dp", "ctx"),
        P("dp", None),
        P(),
        P(),
        P(),
        P(),
        P(),
        P(),
        P(),
        P(),
        P("dp", "ctx", None),
    )
    out_specs = (P("dp", "ctx", None), P(("dp", "ctx")))
    return jax.shard_map(functools.partial(body, mesh.shape["dp"], mesh.shape["ctx"]), mesh=mesh, in_specs=in_specs, out_specs=out_specs, check_vma=False)
```

```python
import functools

import jax
import jax.numpy as jnp
from jax import lax
from jax.experimental import pallas as pl
from jax.experimental.pallas import tpu as pltpu
from jax.sharding import PartitionSpec as P

HEAD = 64
WT = 4
GRID = 14
SW = 7


norm_eps = 1e-06


def extended(block, sides, width):
    for axis, dim in sides:
        count = lax.axis_size(axis)
        forward = [(i, i + 1) for i in range(count - 1)]
        forward.append((count - 1, 0))
        backward = [(target, source) for source, target in forward]
        low = lax.ppermute(
            lax.slice_in_dim(block, block.shape[dim] - width, None, axis=dim), axis, forward
        )
        high = lax.ppermute(lax.slice_in_dim(block, 0, width, axis=dim), axis, backward)
        block = jnp.concatenate([low, block, high], axis=dim)
    return block


def layer_norm(inputs, gain):
    values = inputs.astype(jnp.float32)
    center = values - jnp.mean(values, axis=-1, keepdims=True)
    spread = jnp.mean(center * center, axis=-1, keepdims=True)
    return (center * lax.rsqrt(spread + norm_eps) * gain).astype(jnp.bfloat16)


def softmax_rows(scores):
    highest = jnp.max(scores, axis=-1, keepdims=True)
    raised = jnp.exp(scores - highest)
    return (raised / jnp.sum(raised, axis=-1, keepdims=True)).astype(jnp.bfloat16)


def enc_project(inputs, gain, weight):
    normed = layer_norm(inputs, gain)
    joined = jnp.dot(normed, weight, preferred_element_type=jnp.float32).astype(jnp.bfloat16)
    channels = weight.shape[1] // 3
    return (joined[:, :channels], joined[:, channels : 2 * channels], joined[:, 2 * channels :])


def enc_attend(query, key_all, value_all, live_all):
    query_rows = query.shape[0]
    key_rows = key_all.shape[0]
    head_count = query.shape[1] // HEAD
    query_heads = query.reshape(query_rows, head_count, HEAD).transpose(1, 0, 2)
    key_heads = key_all.reshape(key_rows, head_count, HEAD).transpose(1, 0, 2)
    value_heads = value_all.reshape(key_rows, head_count, HEAD).transpose(1, 0, 2)
    scores = jnp.einsum(
        "hrd,hkd->hrk", query_heads, key_heads, preferred_element_type=jnp.float32
    ) * HEAD ** (-0.5)
    scores = jnp.where(live_all[None, None, :] > 0.5, scores, -1e30)
    weights = softmax_rows(scores)
    mixed = jnp.einsum("hrk,hkd->hrd", weights, value_heads, preferred_element_type=jnp.float32)
    return mixed.transpose(1, 0, 2).reshape(query_rows, -1).astype(jnp.bfloat16)


def enc_finish(inputs, mixed, out_weight, down_weight):
    residual = (
        inputs.astype(jnp.float32) + jnp.dot(mixed, out_weight, preferred_element_type=jnp.float32)
    ).astype(jnp.bfloat16)
    return jnp.dot(residual, down_weight, preferred_element_type=jnp.float32).astype(jnp.bfloat16)


def build_grid(latent, slot_index, token, token_rows):
    base = jnp.broadcast_to(token, (token_rows, token.shape[0]))
    return base.at[slot_index].set(latent.astype(jnp.float32), mode="drop").astype(jnp.bfloat16)


def dec_project(dec_grid, gain, weight):
    normed = layer_norm(dec_grid, gain)
    joined = jnp.dot(normed, weight, preferred_element_type=jnp.float32).astype(jnp.bfloat16)
    channels = weight.shape[1] // 3
    return (joined[:, :channels], joined[:, channels:])


def dec_mix(query, pair_ext, dec_grid, offsets, weight):
    cell_count = GRID * GRID
    steps_own = query.shape[0] // cell_count
    channels = query.shape[1]
    window_span = steps_own + WT
    query_ext = jnp.pad(query.reshape(steps_own, cell_count, channels), ((WT, WT), (0, 0), (0, 0)))
    offset = (offsets[0] + WT - 1) % WT + 1 - WT
    slice_start = offset + WT
    query_win = lax.dynamic_slice_in_dim(query_ext, slice_start, window_span, 0)
    pair_win = lax.dynamic_slice_in_dim(pair_ext, slice_start, window_span, 0)
    joined = jnp.concatenate([query_win, pair_win], -1).reshape(
        window_span, GRID, GRID, 3 * channels
    )
    joined = jnp.roll(joined, (-offsets[1], -offsets[2]), axis=(1, 2))
    side_count = GRID // SW
    windows = joined.reshape(window_span // WT, WT, side_count, SW, side_count, SW, 3 * channels)
    windows = windows.transpose(0, 2, 4, 1, 3, 5, 6).reshape(-1, WT * SW * SW, 3 * channels)
    head_count = channels // HEAD
    window_count = windows.shape[0]
    token_count = windows.shape[1]
    query_heads = (
        windows[..., :channels]
        .reshape(window_count, token_count, head_count, HEAD)
        .transpose(0, 2, 1, 3)
    )
    key_heads = (
        windows[..., channels : 2 * channels]
        .reshape(window_count, token_count, head_count, HEAD)
        .transpose(0, 2, 1, 3)
    )
    value_heads = (
        windows[..., 2 * channels :]
        .reshape(window_count, token_count, head_count, HEAD)
        .transpose(0, 2, 1, 3)
    )
    scores = jnp.einsum(
        "nhqd,nhkd->nhqk", query_heads, key_heads, preferred_element_type=jnp.float32
    ) * HEAD ** (-0.5)
    weights = softmax_rows(scores)
    attended = jnp.einsum(
        "nhqk,nhkd->nhqd", weights, value_heads, preferred_element_type=jnp.float32
    ).astype(jnp.bfloat16)
    attended = attended.transpose(0, 2, 1, 3)
    attended = attended.reshape(window_span // WT, side_count, side_count, WT, SW, SW, channels)
    attended = attended.transpose(0, 3, 1, 4, 2, 5, 6).reshape(window_span, GRID, GRID, channels)
    attended = jnp.roll(attended, (offsets[1], offsets[2]), axis=(1, 2)).reshape(
        window_span, cell_count, channels
    )
    own_rows = lax.dynamic_slice_in_dim(attended, -offset, steps_own, 0).reshape(-1, channels)
    return dec_grid.astype(jnp.float32) + jnp.dot(
        own_rows, weight, preferred_element_type=jnp.float32
    )


def assemble(middle, from_left, from_right):
    total = middle.astype(jnp.float32)
    total = total + from_left.astype(jnp.float32)
    total = total + from_right.astype(jnp.float32)
    return total.astype(jnp.bfloat16)


def flatten(members):
    joined = jnp.concatenate([member.astype(jnp.float32).reshape(-1) for member in members])
    return joined


def plain_body(
    patches,
    vis_index,
    shifts,
    enc_gain,
    enc_qkv,
    enc_out,
    enc_to_dec,
    mask_token,
    dec_gain,
    dec_qkv,
    dec_out,
    dec_cot,
):
    tokens = patches[0]
    slot_index = vis_index[0]
    offsets = shifts[0]
    token_rows = dec_cot.shape[1]
    cell_count = GRID * GRID
    steps_own = token_rows // cell_count
    live_own = (slot_index < token_rows).astype(jnp.bfloat16)
    (query, key_own, value_own), project_pull = jax.vjp(enc_project, tokens, enc_gain, enc_qkv)
    key_all, value_all, live_all = (
        lax.all_gather(key_own, "ctx", axis=0, tiled=True),
        lax.all_gather(value_own, "ctx", axis=0, tiled=True),
        lax.all_gather(live_own, "ctx", axis=0, tiled=True),
    )

    def attend_fn(first, second, third):
        return enc_attend(first, second, third, live_all)

    mixed, attend_pull = jax.vjp(attend_fn, query, key_all, value_all)
    latent, finish_pull = jax.vjp(enc_finish, tokens, mixed, enc_out, enc_to_dec)

    def grid_fn(first, second):
        return build_grid(first, slot_index, second, token_rows)

    dec_grid, grid_pull = jax.vjp(grid_fn, latent, mask_token)
    (dec_query, dec_pair), dproj_pull = jax.vjp(dec_project, dec_grid, dec_gain, dec_qkv)
    pair_cube = dec_pair.reshape(steps_own, cell_count, dec_pair.shape[1])
    pair_ext = extended(pair_cube, (("ctx", 0),), WT)

    def mix_fn(first, second, third, fourth):
        return dec_mix(first, second, third, offsets, fourth)

    decoded, mix_pull = jax.vjp(mix_fn, dec_query, pair_ext, dec_grid, dec_out)
    d_query, d_ext, d_grid_mix, d_dout = mix_pull(dec_cot[0].astype(jnp.float32))
    rim_grads = jnp.concatenate([d_ext[:WT], d_ext[steps_own + WT :]], 0)
    beside_all = extended(rim_grads, (("ctx", 0),), WT)
    from_left = beside_all[:WT]
    from_right = beside_all[3 * WT :]
    d_pair = assemble(d_ext[WT : steps_own + WT], from_left, from_right).reshape(token_rows, -1)
    d_grid_proj, d_dgain, d_dqkv = dproj_pull((d_query, d_pair))
    d_grid = (d_grid_mix.astype(jnp.float32) + d_grid_proj.astype(jnp.float32)).astype(jnp.bfloat16)
    d_latent, d_mask = grid_pull(d_grid)
    d_tokens_res, d_mixed, d_eout, d_e2d = finish_pull(d_latent)
    d_query_enc, d_key_all, d_value_all = attend_pull(d_mixed)
    d_key, d_value = (
        lax.psum_scatter(
            d_key_all.astype(jnp.float32).astype(jnp.bfloat16),
            "ctx",
            scatter_dimension=0,
            tiled=True,
        ).astype(jnp.float32),
        lax.psum_scatter(
            d_value_all.astype(jnp.float32).astype(jnp.bfloat16),
            "ctx",
            scatter_dimension=0,
            tiled=True,
        ).astype(jnp.float32),
    )
    d_tokens_proj, d_egain, d_eqkv = project_pull(
        (d_query_enc, d_key.astype(jnp.bfloat16), d_value.astype(jnp.bfloat16))
    )
    d_patches = (d_tokens_res.astype(jnp.float32) + d_tokens_proj.astype(jnp.float32)).astype(
        jnp.bfloat16
    )[None]
    flat_grads = flatten((d_egain, d_eqkv, d_eout, d_e2d, d_mask, d_dgain, d_dqkv, d_dout))
    clip_share = lax.psum_scatter(
        flat_grads.astype(jnp.bfloat16), "dp", scatter_dimension=0, tiled=True
    )
    summed = lax.psum_scatter(clip_share, "ctx", scatter_dimension=0, tiled=True).astype(
        jnp.float32
    )
    return (d_patches, summed)


LANES = 128
CELLS = GRID * GRID
WINDOW = WT * SW * SW
SIDES = GRID // SW
SPOTS = SIDES * SIDES
PAD = 16
FUSED_SLOTS = 640
NEG = -1e30
F32 = jnp.float32
BF16 = jnp.bfloat16


def mm(left, right):
    return lax.dot_general(left, right, (((1,), (0,)), ((), ())), preferred_element_type=F32)


def mm_nt(left, right):
    return lax.dot_general(left, right, (((1,), (1,)), ((), ())), preferred_element_type=F32)


def mm_tn(left, right):
    return lax.dot_general(left, right, (((0,), (0,)), ((), ())), preferred_element_type=F32)


def normed_rows(values):
    center = values - jnp.mean(values, axis=-1, keepdims=True)
    scale = lax.rsqrt(jnp.mean(center * center, axis=-1, keepdims=True) + norm_eps)
    return center * scale, scale


def norm_back(d_normed, unit, scale, gain):
    d_unit = d_normed * gain
    return scale * (
        d_unit
        - jnp.mean(d_unit, axis=-1, keepdims=True)
        - unit * jnp.mean(d_unit * unit, axis=-1, keepdims=True)
    )


def lane_mask(head, rows, lanes):
    lane = lax.broadcasted_iota(jnp.int32, (rows, lanes), 1)
    return (lane >= head * HEAD) & (lane < (head + 1) * HEAD)


def pack_kernel(shifts, tokens, slots, cot, out):
    rows, width = cot.shape
    front = tokens.shape[1]
    count = slots.shape[1]
    tok = lax.broadcasted_iota(jnp.int32, (rows, LANES), 0)
    lane = lax.broadcasted_iota(jnp.int32, (rows, LANES), 1)
    tok_f = tok.astype(F32)
    step = jnp.floor((tok_f + 0.5) * (1.0 / CELLS))
    cell = tok_f - step * CELLS
    row = jnp.floor((cell + 0.5) * (1.0 / GRID))
    col = cell - row * GRID
    step_at, row_at, col_at = (shifts[0, axis].astype(F32) for axis in range(3))
    row = row - row_at
    row = jnp.where(row < 0, row + GRID, row)
    col = col - col_at
    col = jnp.where(col < 0, col + GRID, col)
    code = jnp.where(row >= SW, float(SIDES), 0.0) + jnp.where(col >= SW, 1.0, 0.0)
    code = code + jnp.where(step >= step_at, float(SPOTS), 0.0)
    hits = (lax.broadcasted_iota(jnp.int32, (rows, count), 0) == slots[...]).astype(F32)
    covered = jnp.sum(hits, axis=1, keepdims=True)
    masked = jnp.where((lane.astype(F32) == code) & (covered < 0.5), 1.0, 0.0).astype(BF16)
    codes = jnp.sum(hits * (code[:, :count] + 1.0), axis=0, keepdims=True)
    hits = hits.astype(BF16)
    out[:, :front] = tokens[...]
    out[:, front : front + width] = mm_tn(hits, cot[...]).astype(BF16)
    sums = mm_tn(masked, cot[...])[: 2 * SPOTS]
    codes = jnp.concatenate([jnp.broadcast_to(codes, (8, count)), jnp.zeros((8, LANES - count), F32)], 1)
    rest = [sums[:, at * LANES : (at + 1) * LANES] for at in range(width // LANES)] + [codes]
    spare = count - 8 * len(rest)
    rest = jnp.concatenate(rest + [jnp.zeros((spare, LANES), F32)], 0)
    out[:, front + width :] = rest.astype(BF16)


def flat_rows(widths):
    places, at = [], 0
    for rows, lanes in widths:
        places.append(at)
        at += rows * lanes // LANES
    return places, at


def store_flat(flat, place, lanes, lane_at, grad):
    for at in range(grad.shape[1] // LANES):
        tile = grad[:, at * LANES : (at + 1) * LANES]
        start = place + lane_at // LANES + at
        if grad.shape[0] == 1:
            flat[start : start + 1, :] = tile
        else:
            flat[pl.ds(start, grad.shape[0], stride=lanes // LANES), :] = tile


def head_rows(widths, n_dp, n_ctx):
    places, total = flat_rows(widths)
    block = total * LANES // (n_dp * n_ctx)
    lanes = widths[1][1]
    most = 0
    for at in range(places[2] * LANES // block):
        first = (at * block - places[1] * LANES) // lanes // PAD * PAD
        last = ((at + 1) * block - places[1] * LANES - 1) // lanes
        most = max(most, last + 1 - first)
    return -(-most // PAD) * PAD


def head_lanes(head, rows, lanes):
    lane = lax.broadcasted_iota(jnp.int32, (rows, lanes), 1)
    return (lane >= head * HEAD) & (lane < (head + 1) * HEAD)


def clip_kernel(n_dp, n_ctx, n_blocks, widths, *refs):
    blocks = refs[:n_blocks]
    enc_gain, mask_token, dec_gain = refs[n_blocks : 3 + n_blocks]
    far = refs[3 + n_blocks : 8 + n_blocks]
    outs = refs[8 + n_blocks :]
    d_patches = outs[0]
    pieces = outs[1 : 1 + n_dp]
    (
        nrm,
        nrm_t,
        qkv,
        weights,
        mixed,
        res,
        dec_in,
        dec_proj,
        hot,
        sums,
        d_mixes,
        d_acc,
        blk_mix,
        blk_cot,
        wide,
        q_stack,
        d_stack,
        p_stack,
        d_p_stack,
        d_query,
        d_keys,
        d_values,
        d_latent,
        d_res,
        d_mixed,
        turned,
        d_scores,
        d_kv_t,
        d_qkv,
        bias,
        enc_qkv_here,
        enc_out_here,
        enc_to_dec_here,
        dec_qkv_here,
        dec_out_here,
        flat,
        part,
        cut,
        sems,
    ) = outs[1 + n_dp :]
    here = (enc_qkv_here, enc_out_here, enc_to_dec_here, dec_qkv_here, dec_out_here)
    loads = [
        pltpu.make_async_copy(far[at], here[at], sems.at[at]) for at in range(len(here))
    ]
    loads[0].start()
    dp_at, ctx_at = lax.axis_index("dp"), lax.axis_index("ctx")
    core = lax.rem(ctx_at, 2)
    count, width = blocks[0].shape[0], enc_gain.shape[1]
    slots = n_ctx * count
    chans = enc_out_here.shape[0]
    dec_chans, dec_width = dec_out_here.shape
    group_lanes = 4 * HEAD
    groups = chans // group_lanes
    scale = HEAD ** (-0.5)
    half = n_ctx // 2
    spread = 2 * SPOTS
    size = count + PAD
    chunk = slots // 2

    tokens_at = slice(0, width)
    cots_at = slice(width, width + dec_width)
    rest_at = slice(width + dec_width, width + dec_width + LANES)

    def pick(at, lanes):
        chip = ctx_at // 2
        block = blocks[at][:, lanes]
        hop = at % half
        if n_blocks == n_ctx or hop not in (1, half - 1):
            return block
        other = blocks[n_ctx + at // half][:, lanes]
        return jnp.where(chip == (half - 1 if hop == 1 else 0), other, block)

    def codes_of(rest):
        at = spread * dec_width // LANES
        return rest[at : at + 8, :count]

    for at in range(n_ctx):
        rows = slice(at * count, (at + 1) * count)
        unit, _ = normed_rows(pick(at, tokens_at).astype(F32))
        nrm[rows, :] = (unit * enc_gain[...]).astype(BF16)
        codes = codes_of(pick(at, rest_at).astype(F32))[:1]
        bias[:, rows] = jnp.broadcast_to(jnp.where(codes > 0.5, 0.0, NEG), (8, count))
    for load in loads[1:]:
        load.start()
    loads[0].wait()

    for at in range(3 * groups):
        lanes = slice(at * group_lanes, (at + 1) * group_lanes)
        qkv[:, lanes] = mm(nrm[...], enc_qkv_here[:, lanes]).astype(BF16)
    nrm_t[:PAD, :] = jnp.zeros((PAD, slots), BF16)
    nrm_t[PAD:, :] = nrm[...].T

    def lanes_of(group):
        return [
            pl.ds(pl.multiple_of(at * chans + group * group_lanes, group_lanes), group_lanes)
            for at in range(3)
        ]

    def attend(group, carry):
        lanes, key_lanes, value_lanes = lanes_of(group)
        keys = qkv[:, key_lanes]
        values = qkv[:, value_lanes]
        for head in range(4):
            own = head_lanes(head, chunk, group_lanes)
            for part in range(slots // chunk):
                rows = slice(part * chunk, (part + 1) * chunk)
                query = jnp.where(own, qkv[rows, lanes].astype(F32) * scale, 0.0).astype(BF16)
                scores = mm_nt(query, keys) + bias[:1]
                raised = jnp.exp(scores - jnp.max(scores, axis=-1, keepdims=True))
                share = (raised * (1.0 / jnp.sum(raised, axis=-1, keepdims=True))).astype(BF16)
                weights[group * 4 + head, rows, :] = share
                mix = mm(share, values)
                if head > 0:
                    mix = jnp.where(own, mix, mixed[rows, lanes].astype(F32))
                mixed[rows, lanes] = mix.astype(BF16)
        return carry

    lax.fori_loop(0, groups, attend, 0)

    loads[1].wait()
    loads[2].wait()
    for at in range(n_ctx):
        rows = slice(at * count, (at + 1) * count)
        out = pick(at, tokens_at).astype(F32) + mm(mixed[rows, :], enc_out_here[...])
        res[rows, :] = out.astype(BF16)
    latent = mm(res[...], enc_to_dec_here[...]).astype(BF16)
    d_latent[...] = latent

    def place(shard, on_core):
        at = shard // 2
        if shard % 2 == 0:
            return at
        return half + (at + on_core) % half

    def rows_of(shard):
        shard = shard % n_ctx
        return slice(shard * count, (shard + 1) * count)

    lane = lax.broadcasted_iota(jnp.int32, (count, LANES), 1).astype(F32)
    square = [lax.broadcasted_iota(jnp.int32, (count, count), axis) for axis in range(2)]
    unity = jnp.where(square[0] == square[1], 1.0, 0.0).astype(BF16)

    def in_time(shard, at):
        dec_in[rows_of(shard), :] = d_latent[rows_of(at), :]
        blk_cot[shard * size : shard * size + count, :] = pick(at, cots_at)
        rest = pick(at, rest_at).astype(F32)
        sums[shard * spread : (shard + 1) * spread, :] = jnp.concatenate(
            [rest[tile * spread : (tile + 1) * spread] for tile in range(dec_width // LANES)], 1
        )
        code = mm_nt(unity, codes_of(rest).astype(BF16))[:, :1] - 1.0
        last = (shard + n_ctx - 1) % n_ctx
        window = code + jnp.where(
            code >= SPOTS, float((shard - 1) * SPOTS), float(last * SPOTS)
        )
        hit = (lane == window) & (code >= 0.0)
        hot[rows_of(shard), :] = jnp.where(hit, 1.0, 0.0).astype(BF16)

    for shard in range(0, n_ctx, 2):
        in_time(shard, place(shard, 0))
    for on_core in range(2):

        @pl.when(core == on_core)
        def _():
            for shard in range(1, n_ctx, 2):
                in_time(shard, place(shard, on_core))

    loads[3].wait()
    loads[4].wait()
    dec_in[slots:, :] = jnp.broadcast_to(mask_token[...], (PAD, dec_width)).astype(BF16)
    for shard in range(n_ctx):
        after = (shard + 1) % n_ctx
        rows_sum = (
            sums[shard * spread + SPOTS : (shard + 1) * spread, :]
            + sums[after * spread : after * spread + SPOTS, :]
        )
        blk_cot[shard * size + count : (shard + 1) * size, :] = jnp.concatenate(
            [rows_sum, jnp.zeros((PAD - SPOTS, dec_width), F32)], 0
        ).astype(BF16)

    dec_unit, dec_scale = normed_rows(dec_in[...].astype(F32))
    dec_nrm = (dec_unit * dec_gain[...]).astype(BF16)
    dec_proj[...] = mm(dec_nrm, dec_qkv_here[...]).astype(BF16)
    d_mixes[...] = mm_nt(blk_cot[...], dec_out_here[...]).astype(BF16)

    pad_row = lax.broadcasted_iota(jnp.int32, (PAD, LANES), 0)
    pad_lane = lax.broadcasted_iota(jnp.int32, (PAD, LANES), 1)
    reach = 3 * count + PAD
    col = lax.broadcasted_iota(jnp.int32, (size, reach), 1)
    owns = [head_lanes(head, size, dec_chans) for head in range(dec_chans // HEAD)]
    tall = len(owns) * size
    mask_rows = slice(slots, slots + PAD)
    query_lanes = slice(0, dec_chans)
    key_lanes = slice(dec_chans, 2 * dec_chans)
    value_lanes = slice(2 * dec_chans, 3 * dec_chans)

    def stack_heads(rows):
        return jnp.concatenate([jnp.where(own, rows, 0.0) for own in owns], 0)

    def unstack_heads(rows):
        total = jnp.where(owns[0], rows[:size], 0.0)
        for head in range(1, len(owns)):
            total = jnp.where(owns[head], rows[head * size : (head + 1) * size], total)
        return total

    def rows_at(shard, rows):
        return pl.ds(pl.multiple_of(shard * rows, PAD), rows)

    def near(ref, shard, lanes, last):
        shards = [lax.rem(shard + n_ctx + step, n_ctx) for step in (-1, 0, 1)]
        return jnp.concatenate([ref[rows_at(at, count), lanes] for at in shards] + [last], 0)

    def keys_of(shard):
        return near(dec_proj, shard, key_lanes, dec_proj[mask_rows, key_lanes])

    def values_of(shard):
        return near(dec_proj, shard, value_lanes, dec_proj[mask_rows, value_lanes])

    def score(shard, here):
        eye = (pad_row + shard * SPOTS == pad_lane) & (pad_row < SPOTS)
        eye = jnp.where(eye, 1.0, 0.0).astype(BF16)
        hot_keys = near(hot, shard, slice(None), jnp.zeros((PAD, LANES), BF16))
        match = mm_nt(jnp.concatenate([hot[rows_at(shard, count), :], eye], 0), hot_keys)
        masked = float(WINDOW) - jnp.sum(match, axis=1, keepdims=True)
        mask_bias = jnp.where(masked > 0.5, jnp.log(jnp.maximum(masked, 1.0)), NEG)
        block_bias = jnp.where(match > 0.5, 0.0, jnp.where(col == 3 * count, mask_bias, NEG))
        queries = jnp.concatenate(
            [dec_proj[rows_at(shard, count), query_lanes], dec_proj[mask_rows, query_lanes]], 0
        )
        queries = stack_heads(queries.astype(F32) * scale).astype(BF16)
        q_stack[here, :] = queries
        d_stack[here, :] = stack_heads(d_mixes[rows_at(shard, size), :].astype(F32)).astype(BF16)
        wide[here, :] = mm_nt(queries, keys_of(shard)) + jnp.concatenate(
            [block_bias] * len(owns), 0
        )

    def soften():
        scores = wide[...]
        raised = jnp.exp(scores - jnp.max(scores, axis=-1, keepdims=True))
        share = raised * (1.0 / jnp.sum(raised, axis=-1, keepdims=True))
        p_stack[...] = share.astype(BF16)

    def mix(shard, here):
        values = values_of(shard)
        blk_mix[rows_at(shard, size), :] = unstack_heads(mm(p_stack[here, :], values)).astype(BF16)
        wide[here, :] = mm_nt(d_stack[here, :], values)

    def soften_back():
        share = p_stack[...].astype(F32)
        d_share = wide[...]
        delta = jnp.sum(d_share * share, axis=-1, keepdims=True)
        d_p_stack[...] = (share * (d_share - delta)).astype(BF16)

    def mix_back(shard, here):
        d_score = d_p_stack[here, :]
        d_query[rows_at(shard, size), :] = unstack_heads(mm(d_score, keys_of(shard))) * scale
        d_keys[shard] = mm_tn(d_score, q_stack[here, :]).astype(BF16)
        d_values[shard] = mm_tn(p_stack[here, :], d_stack[here, :]).astype(BF16)

    at_once = 4 if n_ctx % 4 == 0 else 2

    def some_shards(at, carry):
        both = [(at_once * at + one, slice(one * tall, (one + 1) * tall)) for one in range(at_once)]
        for shard, here in both:
            score(shard, here)
        soften()
        for shard, here in both:
            mix(shard, here)
        soften_back()
        for shard, here in both:
            mix_back(shard, here)
        return carry

    lax.fori_loop(0, n_ctx // at_once, some_shards, 0)

    mask_d_query = jnp.zeros((1, dec_chans), F32)
    mask_d_pair = [jnp.zeros((1, dec_chans), F32) for _ in range(2)]
    for shard in range(n_ctx):
        rows = rows_of(shard)
        d_acc[rows, query_lanes] = d_query[shard * size : shard * size + count, :].astype(BF16)
        mask_d_query += jnp.sum(
            d_query[shard * size + count : shard * size + count + SPOTS, :], 0, keepdims=True
        )
        for at, (lanes, ref) in enumerate(((key_lanes, d_keys), (value_lanes, d_values))):
            before, after = (shard + n_ctx - 1) % n_ctx, (shard + 1) % n_ctx
            total = (
                ref[before, 2 * count : 3 * count, :].astype(F32)
                + ref[shard, count : 2 * count, :].astype(F32)
                + ref[after, :count, :].astype(F32)
            )
            d_acc[rows, lanes] = total.astype(BF16)
            mask_d_pair[at] += ref[shard, 3 * count :, :].astype(F32)[:1]
    first = lax.broadcasted_iota(jnp.int32, (PAD, 3 * dec_chans), 0) == 0
    mask_d = jnp.concatenate([mask_d_query] + mask_d_pair, 1)
    d_acc[mask_rows, :] = jnp.where(first, mask_d, 0.0).astype(BF16)

    d_dec_proj = d_acc[...]
    d_dec_nrm = mm_nt(d_dec_proj, dec_qkv_here[...])
    g_dec_qkv = mm_tn(dec_nrm, d_dec_proj)
    g_dec_out = mm_tn(blk_mix[...], blk_cot[...])
    g_dec_gain = jnp.sum(d_dec_nrm * dec_unit, axis=0, keepdims=True)
    d_dec_in = norm_back(d_dec_nrm, dec_unit, dec_scale, dec_gain[...])
    g_mask = jnp.sum(sums[...], axis=0, keepdims=True) + d_dec_in[slots : slots + 1]
    for shard in range(n_ctx):
        cot = blk_cot[shard * size : shard * size + count, :].astype(F32)
        back = d_dec_in[shard * count : (shard + 1) * count].astype(BF16).astype(F32)
        dec_in[rows_of(shard), :] = (cot + back).astype(BF16)
    for on_core in range(2):

        @pl.when(core == on_core)
        def _():
            for shard in range(n_ctx):
                d_latent[rows_of(place(shard, on_core)), :] = dec_in[rows_of(shard), :]

    d_res[...] = mm_nt(d_latent[...], enc_to_dec_here[...]).astype(BF16)
    d_mixed[...] = mm_nt(d_res[...], enc_out_here[...]).astype(BF16)

    places, total = flat_rows(widths)
    block_rows = 2 * total // (n_dp * n_ctx)
    late_at = places[2]

    def store(which, lane_at, grad):
        store_flat(flat, places[which] - late_at, widths[which][1], lane_at, grad)

    store(2, 0, mm_tn(mixed[...], d_res[...]))
    store(3, 0, mm_tn(res[...], d_latent[...]))
    store(4, 0, g_mask)
    store(5, 0, g_dec_gain)
    store(6, 0, g_dec_qkv)
    store(7, 0, g_dec_out)

    def attend_back(group, carry):
        lanes, key_lanes, value_lanes = lanes_of(group)
        turned[:group_lanes, :] = qkv[:, lanes].T
        turned[group_lanes:, :] = d_mixed[:, lanes].T
        keys = qkv[:, key_lanes]
        values = qkv[:, value_lanes]
        for head in range(4):
            own = head_lanes(head, chunk, group_lanes)
            at_head = group * 4 + head
            for part in range(slots // chunk):
                rows = slice(part * chunk, (part + 1) * chunk)
                cot = jnp.where(own, d_mixed[rows, lanes].astype(F32), 0.0)
                delta = jnp.sum(cot * mixed[rows, lanes].astype(F32), axis=-1, keepdims=True)
                d_share = mm_nt(cot.astype(BF16), values)
                d_score = weights[at_head, rows, :].astype(F32) * (d_share - delta)
                d_score = d_score.astype(BF16)
                d_scores[head % 2, rows, :] = d_score
                d_query = mm(d_score, keys) * scale
                if head > 0:
                    d_query = jnp.where(own, d_query, d_qkv[rows, lanes].astype(F32))
                d_qkv[rows, lanes] = d_query.astype(BF16)
            to_key = pl.ds(pl.multiple_of(at_head * HEAD, HEAD), HEAD)
            to_value = pl.ds(pl.multiple_of(chans + at_head * HEAD, HEAD), HEAD)
            query_t = turned[head * HEAD : (head + 1) * HEAD, :]
            cot_t = turned[group_lanes + head * HEAD : group_lanes + (head + 1) * HEAD, :]
            d_kv_t[to_key, :] = (mm(query_t, d_scores[head % 2]) * scale).astype(BF16)
            d_kv_t[to_value, :] = mm(cot_t, weights[at_head]).astype(BF16)
        return carry

    lax.fori_loop(0, groups, attend_back, 0)
    d_qkv[:, chans:] = d_kv_t[...].T

    d_nrm = mm_nt(d_qkv[...], enc_qkv_here[...])
    gain_grad = jnp.sum(d_nrm * nrm[...].astype(F32), axis=0, keepdims=True) / enc_gain[...]
    unit, unit_scale = normed_rows(blocks[0][:, tokens_at].astype(F32))
    d_own = norm_back(d_nrm[:count], unit, unit_scale, enc_gain[...]).astype(BF16).astype(F32)
    d_patches[...] = (d_res[:count, :].astype(F32) + d_own).astype(BF16)

    piece_rows = cut.shape[1]
    some = head_rows(widths, n_dp, n_ctx)
    lanes_all = 3 * chans
    tiles = lanes_all // LANES

    def cut_at(ref, start, to):
        slot = lax.rem(to - dp_at + n_dp, n_dp)
        shift = lax.rem(start, 8)
        base = start - shift
        for small in range(8):

            @pl.when(shift == small)
            def _():
                rows = ref[pl.ds(pl.multiple_of(base, 8), piece_rows + 8), :]
                cut[slot] = rows[small : small + piece_rows].astype(BF16)

    def cut_early(to, carry):
        start = (to * n_ctx + ctx_at) * block_rows // 2
        first = (start - places[1] + PAD * tiles) // tiles // PAD * PAD
        rows = nrm_t[pl.ds(pl.multiple_of(first, PAD), some), :]
        store_flat(part, 0, lanes_all, 0, mm(rows, d_qkv[...]))
        begin = start - places[1] + (PAD - first) * tiles

        @pl.when(start == 0)
        def _():
            store_flat(part, PAD * tiles - places[1], width, 0, gain_grad)

        cut_at(part, begin, to)
        return carry

    def cut_late(to, carry):
        cut_at(flat, (to * n_ctx + ctx_at) * block_rows // 2 - late_at, to)
        return carry

    first_late = late_at * n_dp // total
    lax.fori_loop(0, first_late, cut_early, 0)
    lax.fori_loop(first_late, n_dp, cut_late, 0)
    for at in range(n_dp):
        pieces[at][...] = cut[at]


def join_kernel(*refs):
    out = refs[-1]
    total = refs[0][...].astype(F32)
    for ref in refs[1:-1]:
        total = total + ref[...].astype(F32)
    rows = total.shape[0]
    lane = lax.broadcasted_iota(jnp.int32, (rows, LANES), 1)
    turned = pltpu.roll(total, LANES // 2, 1)
    turned = jnp.where(lane < LANES // 2, turned, pltpu.roll(turned, rows - 1, 0))
    total = jnp.where(lax.rem(lax.axis_index("ctx"), 2) == 1, turned, total)
    full = out.shape[0] // (8 * LANES) * 8
    left = out.shape[0] - full * LANES
    out[: full * LANES] = total[:full].reshape(full * LANES)
    if left > 0:
        out[full * LANES :] = total[full : full + 8].reshape(8 * LANES)[:left]


def fused_body(
    n_dp,
    n_ctx,
    patches,
    vis_index,
    shifts,
    enc_gain,
    enc_qkv,
    enc_out,
    enc_to_dec,
    mask_token,
    dec_gain,
    dec_qkv,
    dec_out,
    dec_cot,
):
    tokens = patches[0]
    params = (enc_gain, enc_qkv, enc_out, enc_to_dec, mask_token, dec_gain, dec_qkv, dec_out)
    widths = [(1,) * (2 - param.ndim) + param.shape for param in params]
    half = n_ctx // 2

    def by_hops(block):
        def shift(array, hops, chips):
            pairs = [((chip + hops) % half, chip) for chip in chips]
            turn = [(2 * pair[0] + core, 2 * pair[1] + core) for pair in pairs for core in range(2)]
            return lax.ppermute(array, "ctx", turn)

        def swap(array, chips):
            return lax.ppermute(
                array, "ctx", [(2 * chip + core, 2 * chip + 1 - core) for chip in chips for core in range(2)]
            )

        every = range(half)
        if half != 4:
            near = [block] + [shift(block, step, every) for step in range(1, half)]
            return near + [swap(other, every) for other in near]
        where = (every, every[:-1], every, every[1:], (0, half - 1))
        middle = shift(block, 2, every)
        first, last = shift(block, 1, where[1]), shift(block, 3, where[3])
        ends = lax.ppermute(
            middle, "ctx", [(2 * a + core, 2 * b + core) for a, b in ((1, 0), (2, 3)) for core in range(2)]
        )
        near = [block, first, middle, last, ends]
        far = [swap(other, chips) for other, chips in zip(near, where)]
        return near[:4] + far[:4] + [near[4], far[4]]

    blocks = by_hops(call_pack(shifts, tokens, vis_index, dec_cot[0]))
    d_patches, *pieces = call_clip(n_dp, n_ctx, widths, blocks, params)
    got = [pieces[0]]
    for step in range(1, n_dp):
        turn = [(at, (at + step) % n_dp) for at in range(n_dp)]
        got.append(lax.ppermute(pieces[step], "dp", turn))
    share = flat_rows(widths)[1] * LANES // (n_dp * n_ctx)
    return d_patches[None], call_join(got, share)


def piece_shape(n_dp, n_ctx, widths):
    share = flat_rows(widths)[1] * LANES // (n_dp * n_ctx)
    rows = -(-(share + LANES // 2) // LANES)
    return jax.ShapeDtypeStruct((-(-rows // PAD) * PAD, LANES), BF16)


IN_VMEM = pl.BlockSpec(memory_space=pltpu.VMEM)
IN_SMEM = pl.BlockSpec(memory_space=pltpu.SMEM)
ANYWHERE = pl.BlockSpec(memory_space=pl.ANY)


def call_pack(shifts, tokens, vis_index, cot):
    count, width = tokens.shape
    return pl.pallas_call(
        pack_kernel,
        out_shape=jax.ShapeDtypeStruct((count, width + cot.shape[1] + LANES), BF16),
        in_specs=[IN_SMEM, IN_VMEM, IN_VMEM, IN_VMEM],
        out_specs=IN_VMEM,
        name="pack",
    )(shifts, tokens, vis_index, cot)


def call_clip(n_dp, n_ctx, widths, blocks, params):
    enc_gain, enc_qkv, enc_out, enc_to_dec, mask_token, dec_gain, dec_qkv, dec_out = params
    count, width = blocks[0].shape[0], enc_gain.shape[0]
    slots = n_ctx * count
    chans = enc_out.shape[0]
    dec_chans, dec_width = dec_out.shape
    places, total = flat_rows(widths)
    piece = piece_shape(n_dp, n_ctx, widths)
    part_rows = (head_rows(widths, n_dp, n_ctx) + PAD) * 3 * chans // LANES + 2 * PAD
    size = count + PAD
    tall = dec_chans // HEAD * size
    reach = 3 * count + PAD
    matrices = (enc_qkv, enc_out, enc_to_dec, dec_qkv, dec_out)
    return pl.pallas_call(
        functools.partial(clip_kernel, n_dp, n_ctx, len(blocks), widths),
        out_shape=[jax.ShapeDtypeStruct((count, width), BF16)] + [piece] * n_dp,
        in_specs=[IN_VMEM] * (len(blocks) + 3) + [ANYWHERE] * len(matrices),
        out_specs=[IN_VMEM] * (1 + n_dp),
        scratch_shapes=[
            pltpu.VMEM((slots, width), BF16),
            pltpu.VMEM((PAD + width, slots), BF16),
            pltpu.VMEM((slots, 3 * chans), BF16),
            pltpu.VMEM((chans // HEAD, slots, slots), BF16),
            pltpu.VMEM((slots, chans), BF16),
            pltpu.VMEM((slots, width), BF16),
            pltpu.VMEM((slots + PAD, dec_width), BF16),
            pltpu.VMEM((slots + PAD, 3 * dec_chans), BF16),
            pltpu.VMEM((slots, LANES), BF16),
            pltpu.VMEM((n_ctx * 2 * SPOTS, dec_width), F32),
            pltpu.VMEM((n_ctx * size, dec_chans), BF16),
            pltpu.VMEM((slots + PAD, 3 * dec_chans), BF16),
            pltpu.VMEM((n_ctx * size, dec_chans), BF16),
            pltpu.VMEM((n_ctx * size, dec_width), BF16),
            pltpu.VMEM((4 * tall, reach), F32),
            pltpu.VMEM((4 * tall, dec_chans), BF16),
            pltpu.VMEM((4 * tall, dec_chans), BF16),
            pltpu.VMEM((4 * tall, reach), BF16),
            pltpu.VMEM((4 * tall, reach), BF16),
            pltpu.VMEM((n_ctx * size, dec_chans), F32),
            pltpu.VMEM((n_ctx, reach, dec_chans), BF16),
            pltpu.VMEM((n_ctx, reach, dec_chans), BF16),
            pltpu.VMEM((slots, dec_width), BF16),
            pltpu.VMEM((slots, width), BF16),
            pltpu.VMEM((slots, chans), BF16),
            pltpu.VMEM((8 * HEAD, slots), BF16),
            pltpu.VMEM((2, slots, slots), BF16),
            pltpu.VMEM((2 * chans, slots), BF16),
            pltpu.VMEM((slots, 3 * chans), BF16),
            pltpu.VMEM((8, slots), F32),
        ]
        + [pltpu.VMEM(matrix.shape, BF16) for matrix in matrices]
        + [
            pltpu.VMEM((total - places[2] + 2 * PAD, LANES), F32),
            pltpu.VMEM((part_rows, LANES), F32),
            pltpu.VMEM((n_dp,) + piece.shape, BF16),
            pltpu.SemaphoreType.DMA((len(matrices),)),
        ],
        compiler_params=pltpu.CompilerParams(vmem_limit_bytes=VMEM_BYTES),
        cost_estimate=pl.CostEstimate(
            flops=40 * 10**9, bytes_accessed=16 * 2**20, transcendentals=0
        ),
        name="clip",
    )(
        *blocks,
        enc_gain[None],
        mask_token[None],
        dec_gain[None],
        *matrices,
    )


def call_join(blocks, share):
    return pl.pallas_call(
        join_kernel,
        out_shape=jax.ShapeDtypeStruct((share,), F32),
        in_specs=[IN_VMEM] * len(blocks),
        out_specs=IN_VMEM,
        compiler_params=pltpu.CompilerParams(vmem_limit_bytes=SMALL_VMEM_BYTES),
        name="join",
    )(*blocks)


SMALL_VMEM_BYTES = 8 * 1024 * 1024
VMEM_BYTES = 56 * 1024 * 1024


def body(n_dp, n_ctx, patches, vis_index, *rest):
    enc_qkv = rest[2]
    dec_cot = rest[-1]
    head = enc_qkv.shape[0] * (1 + enc_qkv.shape[1])
    length = sum(param.size for param in rest[1:-1])
    small = n_ctx * patches.shape[1] <= FUSED_SLOTS
    whole = head * n_dp % length == 0 and dec_cot.shape[1] == WT * CELLS
    if small and n_ctx % 2 == 0 and whole:
        return fused_body(n_dp, n_ctx, patches, vis_index, *rest)
    return plain_body(patches, vis_index, *rest)


def solution(mesh):
    in_specs = (
        P("dp", "ctx", None),
        P("dp", "ctx"),
        P("dp", None),
        P(),
        P(),
        P(),
        P(),
        P(),
        P(),
        P(),
        P(),
        P("dp", "ctx", None),
    )
    out_specs = (P("dp", "ctx", None), P(("dp", "ctx")))
    return jax.shard_map(functools.partial(body, mesh.shape["dp"], mesh.shape["ctx"]), mesh=mesh, in_specs=in_specs, out_specs=out_specs, check_vma=False)
```

```python
import functools

import jax
import jax.numpy as jnp
from jax import lax
from jax.experimental import pallas as pl
from jax.experimental.pallas import tpu as pltpu
from jax.sharding import PartitionSpec as P

HEAD = 64
WT = 4
GRID = 14
SW = 7


norm_eps = 1e-06


def extended(block, sides, width):
    for axis, dim in sides:
        count = lax.axis_size(axis)
        forward = [(i, i + 1) for i in range(count - 1)]
        forward.append((count - 1, 0))
        backward = [(target, source) for source, target in forward]
        low = lax.ppermute(
            lax.slice_in_dim(block, block.shape[dim] - width, None, axis=dim), axis, forward
        )
        high = lax.ppermute(lax.slice_in_dim(block, 0, width, axis=dim), axis, backward)
        block = jnp.concatenate([low, block, high], axis=dim)
    return block


def layer_norm(inputs, gain):
    values = inputs.astype(jnp.float32)
    center = values - jnp.mean(values, axis=-1, keepdims=True)
    spread = jnp.mean(center * center, axis=-1, keepdims=True)
    return (center * lax.rsqrt(spread + norm_eps) * gain).astype(jnp.bfloat16)


def softmax_rows(scores):
    highest = jnp.max(scores, axis=-1, keepdims=True)
    raised = jnp.exp(scores - highest)
    return (raised / jnp.sum(raised, axis=-1, keepdims=True)).astype(jnp.bfloat16)


def enc_project(inputs, gain, weight):
    normed = layer_norm(inputs, gain)
    joined = jnp.dot(normed, weight, preferred_element_type=jnp.float32).astype(jnp.bfloat16)
    channels = weight.shape[1] // 3
    return (joined[:, :channels], joined[:, channels : 2 * channels], joined[:, 2 * channels :])


def enc_attend(query, key_all, value_all, live_all):
    query_rows = query.shape[0]
    key_rows = key_all.shape[0]
    head_count = query.shape[1] // HEAD
    query_heads = query.reshape(query_rows, head_count, HEAD).transpose(1, 0, 2)
    key_heads = key_all.reshape(key_rows, head_count, HEAD).transpose(1, 0, 2)
    value_heads = value_all.reshape(key_rows, head_count, HEAD).transpose(1, 0, 2)
    scores = jnp.einsum(
        "hrd,hkd->hrk", query_heads, key_heads, preferred_element_type=jnp.float32
    ) * HEAD ** (-0.5)
    scores = jnp.where(live_all[None, None, :] > 0.5, scores, -1e30)
    weights = softmax_rows(scores)
    mixed = jnp.einsum("hrk,hkd->hrd", weights, value_heads, preferred_element_type=jnp.float32)
    return mixed.transpose(1, 0, 2).reshape(query_rows, -1).astype(jnp.bfloat16)


def enc_finish(inputs, mixed, out_weight, down_weight):
    residual = (
        inputs.astype(jnp.float32) + jnp.dot(mixed, out_weight, preferred_element_type=jnp.float32)
    ).astype(jnp.bfloat16)
    return jnp.dot(residual, down_weight, preferred_element_type=jnp.float32).astype(jnp.bfloat16)


def build_grid(latent, slot_index, token, token_rows):
    base = jnp.broadcast_to(token, (token_rows, token.shape[0]))
    return base.at[slot_index].set(latent.astype(jnp.float32), mode="drop").astype(jnp.bfloat16)


def dec_project(dec_grid, gain, weight):
    normed = layer_norm(dec_grid, gain)
    joined = jnp.dot(normed, weight, preferred_element_type=jnp.float32).astype(jnp.bfloat16)
    channels = weight.shape[1] // 3
    return (joined[:, :channels], joined[:, channels:])


def dec_mix(query, pair_ext, dec_grid, offsets, weight):
    cell_count = GRID * GRID
    steps_own = query.shape[0] // cell_count
    channels = query.shape[1]
    window_span = steps_own + WT
    query_ext = jnp.pad(query.reshape(steps_own, cell_count, channels), ((WT, WT), (0, 0), (0, 0)))
    offset = (offsets[0] + WT - 1) % WT + 1 - WT
    slice_start = offset + WT
    query_win = lax.dynamic_slice_in_dim(query_ext, slice_start, window_span, 0)
    pair_win = lax.dynamic_slice_in_dim(pair_ext, slice_start, window_span, 0)
    joined = jnp.concatenate([query_win, pair_win], -1).reshape(
        window_span, GRID, GRID, 3 * channels
    )
    joined = jnp.roll(joined, (-offsets[1], -offsets[2]), axis=(1, 2))
    side_count = GRID // SW
    windows = joined.reshape(window_span // WT, WT, side_count, SW, side_count, SW, 3 * channels)
    windows = windows.transpose(0, 2, 4, 1, 3, 5, 6).reshape(-1, WT * SW * SW, 3 * channels)
    head_count = channels // HEAD
    window_count = windows.shape[0]
    token_count = windows.shape[1]
    query_heads = (
        windows[..., :channels]
        .reshape(window_count, token_count, head_count, HEAD)
        .transpose(0, 2, 1, 3)
    )
    key_heads = (
        windows[..., channels : 2 * channels]
        .reshape(window_count, token_count, head_count, HEAD)
        .transpose(0, 2, 1, 3)
    )
    value_heads = (
        windows[..., 2 * channels :]
        .reshape(window_count, token_count, head_count, HEAD)
        .transpose(0, 2, 1, 3)
    )
    scores = jnp.einsum(
        "nhqd,nhkd->nhqk", query_heads, key_heads, preferred_element_type=jnp.float32
    ) * HEAD ** (-0.5)
    weights = softmax_rows(scores)
    attended = jnp.einsum(
        "nhqk,nhkd->nhqd", weights, value_heads, preferred_element_type=jnp.float32
    ).astype(jnp.bfloat16)
    attended = attended.transpose(0, 2, 1, 3)
    attended = attended.reshape(window_span // WT, side_count, side_count, WT, SW, SW, channels)
    attended = attended.transpose(0, 3, 1, 4, 2, 5, 6).reshape(window_span, GRID, GRID, channels)
    attended = jnp.roll(attended, (offsets[1], offsets[2]), axis=(1, 2)).reshape(
        window_span, cell_count, channels
    )
    own_rows = lax.dynamic_slice_in_dim(attended, -offset, steps_own, 0).reshape(-1, channels)
    return dec_grid.astype(jnp.float32) + jnp.dot(
        own_rows, weight, preferred_element_type=jnp.float32
    )


def assemble(middle, from_left, from_right):
    total = middle.astype(jnp.float32)
    total = total + from_left.astype(jnp.float32)
    total = total + from_right.astype(jnp.float32)
    return total.astype(jnp.bfloat16)


def flatten(members):
    joined = jnp.concatenate([member.astype(jnp.float32).reshape(-1) for member in members])
    return joined


def plain_body(
    patches,
    vis_index,
    shifts,
    enc_gain,
    enc_qkv,
    enc_out,
    enc_to_dec,
    mask_token,
    dec_gain,
    dec_qkv,
    dec_out,
    dec_cot,
):
    tokens = patches[0]
    slot_index = vis_index[0]
    offsets = shifts[0]
    token_rows = dec_cot.shape[1]
    cell_count = GRID * GRID
    steps_own = token_rows // cell_count
    live_own = (slot_index < token_rows).astype(jnp.bfloat16)
    (query, key_own, value_own), project_pull = jax.vjp(enc_project, tokens, enc_gain, enc_qkv)
    key_all, value_all, live_all = (
        lax.all_gather(key_own, "ctx", axis=0, tiled=True),
        lax.all_gather(value_own, "ctx", axis=0, tiled=True),
        lax.all_gather(live_own, "ctx", axis=0, tiled=True),
    )

    def attend_fn(first, second, third):
        return enc_attend(first, second, third, live_all)

    mixed, attend_pull = jax.vjp(attend_fn, query, key_all, value_all)
    latent, finish_pull = jax.vjp(enc_finish, tokens, mixed, enc_out, enc_to_dec)

    def grid_fn(first, second):
        return build_grid(first, slot_index, second, token_rows)

    dec_grid, grid_pull = jax.vjp(grid_fn, latent, mask_token)
    (dec_query, dec_pair), dproj_pull = jax.vjp(dec_project, dec_grid, dec_gain, dec_qkv)
    pair_cube = dec_pair.reshape(steps_own, cell_count, dec_pair.shape[1])
    pair_ext = extended(pair_cube, (("ctx", 0),), WT)

    def mix_fn(first, second, third, fourth):
        return dec_mix(first, second, third, offsets, fourth)

    decoded, mix_pull = jax.vjp(mix_fn, dec_query, pair_ext, dec_grid, dec_out)
    d_query, d_ext, d_grid_mix, d_dout = mix_pull(dec_cot[0].astype(jnp.float32))
    rim_grads = jnp.concatenate([d_ext[:WT], d_ext[steps_own + WT :]], 0)
    beside_all = extended(rim_grads, (("ctx", 0),), WT)
    from_left = beside_all[:WT]
    from_right = beside_all[3 * WT :]
    d_pair = assemble(d_ext[WT : steps_own + WT], from_left, from_right).reshape(token_rows, -1)
    d_grid_proj, d_dgain, d_dqkv = dproj_pull((d_query, d_pair))
    d_grid = (d_grid_mix.astype(jnp.float32) + d_grid_proj.astype(jnp.float32)).astype(jnp.bfloat16)
    d_latent, d_mask = grid_pull(d_grid)
    d_tokens_res, d_mixed, d_eout, d_e2d = finish_pull(d_latent)
    d_query_enc, d_key_all, d_value_all = attend_pull(d_mixed)
    d_key, d_value = (
        lax.psum_scatter(
            d_key_all.astype(jnp.float32).astype(jnp.bfloat16),
            "ctx",
            scatter_dimension=0,
            tiled=True,
        ).astype(jnp.float32),
        lax.psum_scatter(
            d_value_all.astype(jnp.float32).astype(jnp.bfloat16),
            "ctx",
            scatter_dimension=0,
            tiled=True,
        ).astype(jnp.float32),
    )
    d_tokens_proj, d_egain, d_eqkv = project_pull(
        (d_query_enc, d_key.astype(jnp.bfloat16), d_value.astype(jnp.bfloat16))
    )
    d_patches = (d_tokens_res.astype(jnp.float32) + d_tokens_proj.astype(jnp.float32)).astype(
        jnp.bfloat16
    )[None]
    flat_grads = flatten((d_egain, d_eqkv, d_eout, d_e2d, d_mask, d_dgain, d_dqkv, d_dout))
    clip_share = lax.psum_scatter(
        flat_grads.astype(jnp.bfloat16), "dp", scatter_dimension=0, tiled=True
    )
    summed = lax.psum_scatter(clip_share, "ctx", scatter_dimension=0, tiled=True).astype(
        jnp.float32
    )
    return (d_patches, summed)


LANES = 128
CELLS = GRID * GRID
WINDOW = WT * SW * SW
SIDES = GRID // SW
SPOTS = SIDES * SIDES
PAD = 16
FUSED_SLOTS = 640
NEG = -1e30
F32 = jnp.float32
BF16 = jnp.bfloat16


def mm(left, right):
    return lax.dot_general(left, right, (((1,), (0,)), ((), ())), preferred_element_type=F32)


def mm_nt(left, right):
    return lax.dot_general(left, right, (((1,), (1,)), ((), ())), preferred_element_type=F32)


def mm_tn(left, right):
    return lax.dot_general(left, right, (((0,), (0,)), ((), ())), preferred_element_type=F32)


def normed_rows(values):
    center = values - jnp.mean(values, axis=-1, keepdims=True)
    scale = lax.rsqrt(jnp.mean(center * center, axis=-1, keepdims=True) + norm_eps)
    return center * scale, scale


def norm_back(d_normed, unit, scale, gain):
    d_unit = d_normed * gain
    return scale * (
        d_unit
        - jnp.mean(d_unit, axis=-1, keepdims=True)
        - unit * jnp.mean(d_unit * unit, axis=-1, keepdims=True)
    )


def lane_mask(head, rows, lanes):
    lane = lax.broadcasted_iota(jnp.int32, (rows, lanes), 1)
    return (lane >= head * HEAD) & (lane < (head + 1) * HEAD)


def pack_kernel(shifts, tokens, slots, cot, out):
    rows, width = cot.shape
    front = tokens.shape[1]
    count = slots.shape[1]
    tok = lax.broadcasted_iota(jnp.int32, (rows, LANES), 0)
    lane = lax.broadcasted_iota(jnp.int32, (rows, LANES), 1)
    tok_f = tok.astype(F32)
    step = jnp.floor((tok_f + 0.5) * (1.0 / CELLS))
    cell = tok_f - step * CELLS
    row = jnp.floor((cell + 0.5) * (1.0 / GRID))
    col = cell - row * GRID
    step_at, row_at, col_at = (shifts[0, axis].astype(F32) for axis in range(3))
    row = row - row_at
    row = jnp.where(row < 0, row + GRID, row)
    col = col - col_at
    col = jnp.where(col < 0, col + GRID, col)
    code = jnp.where(row >= SW, float(SIDES), 0.0) + jnp.where(col >= SW, 1.0, 0.0)
    code = code + jnp.where(step >= step_at, float(SPOTS), 0.0)
    hits = (lax.broadcasted_iota(jnp.int32, (rows, count), 0) == slots[...]).astype(F32)
    covered = jnp.sum(hits, axis=1, keepdims=True)
    masked = jnp.where((lane.astype(F32) == code) & (covered < 0.5), 1.0, 0.0).astype(BF16)
    codes = jnp.sum(hits * (code[:, :count] + 1.0), axis=0, keepdims=True)
    hits = hits.astype(BF16)
    out[:, :front] = tokens[...]
    out[:, front : front + width] = mm_tn(hits, cot[...]).astype(BF16)
    sums = mm_tn(masked, cot[...])[: 2 * SPOTS]
    codes = jnp.concatenate([jnp.broadcast_to(codes, (8, count)), jnp.zeros((8, LANES - count), F32)], 1)
    rest = [sums[:, at * LANES : (at + 1) * LANES] for at in range(width // LANES)] + [codes]
    spare = count - 8 * len(rest)
    rest = jnp.concatenate(rest + [jnp.zeros((spare, LANES), F32)], 0)
    out[:, front + width :] = rest.astype(BF16)


def flat_rows(widths):
    places, at = [], 0
    for rows, lanes in widths:
        places.append(at)
        at += rows * lanes // LANES
    return places, at


def store_flat(flat, place, lanes, lane_at, grad):
    for at in range(grad.shape[1] // LANES):
        tile = grad[:, at * LANES : (at + 1) * LANES]
        start = place + lane_at // LANES + at
        if grad.shape[0] == 1:
            flat[start : start + 1, :] = tile
        else:
            flat[pl.ds(start, grad.shape[0], stride=lanes // LANES), :] = tile


def head_rows(widths, n_dp, n_ctx):
    places, total = flat_rows(widths)
    block = total * LANES // (n_dp * n_ctx)
    lanes = widths[1][1]
    most = 0
    for at in range(places[2] * LANES // block):
        first = (at * block - places[1] * LANES) // lanes // PAD * PAD
        last = ((at + 1) * block - places[1] * LANES - 1) // lanes
        most = max(most, last + 1 - first)
    return -(-most // PAD) * PAD


def head_lanes(head, rows, lanes):
    lane = lax.broadcasted_iota(jnp.int32, (rows, lanes), 1)
    return (lane >= head * HEAD) & (lane < (head + 1) * HEAD)


def clip_kernel(n_dp, n_ctx, n_blocks, widths, *refs):
    blocks = refs[:n_blocks]
    enc_gain, mask_token, dec_gain = refs[n_blocks : 3 + n_blocks]
    far = refs[3 + n_blocks : 8 + n_blocks]
    outs = refs[8 + n_blocks :]
    d_patches = outs[0]
    pieces = outs[1 : 1 + n_dp]
    (
        nrm,
        nrm_t,
        qkv,
        weights,
        mixed,
        res,
        dec_in,
        dec_proj,
        hot,
        sums,
        d_mixes,
        d_acc,
        blk_mix,
        blk_cot,
        wide,
        q_stack,
        d_stack,
        p_stack,
        d_p_stack,
        d_query,
        d_keys,
        d_values,
        d_latent,
        d_res,
        d_mixed,
        turned,
        d_scores,
        d_kv_t,
        d_qkv,
        bias,
        enc_qkv_here,
        enc_out_here,
        enc_to_dec_here,
        dec_qkv_here,
        dec_out_here,
        flat,
        part,
        cut,
        sems,
    ) = outs[1 + n_dp :]
    here = (enc_qkv_here, enc_out_here, enc_to_dec_here, dec_qkv_here, dec_out_here)
    loads = [
        pltpu.make_async_copy(far[at], here[at], sems.at[at]) for at in range(len(here))
    ]
    loads[0].start()
    dp_at, ctx_at = lax.axis_index("dp"), lax.axis_index("ctx")
    core = lax.rem(ctx_at, 2)
    count, width = blocks[0].shape[0], enc_gain.shape[1]
    slots = n_ctx * count
    chans = enc_out_here.shape[0]
    dec_chans, dec_width = dec_out_here.shape
    group_lanes = 4 * HEAD
    groups = chans // group_lanes
    scale = HEAD ** (-0.5)
    half = n_ctx // 2
    spread = 2 * SPOTS
    size = count + PAD
    chunk = slots // 2

    tokens_at = slice(0, width)
    cots_at = slice(width, width + dec_width)
    rest_at = slice(width + dec_width, width + dec_width + LANES)

    def pick(at, lanes):
        chip = ctx_at // 2
        block = blocks[at][:, lanes]
        hop = at % half
        if n_blocks == n_ctx or hop not in (1, half - 1):
            return block
        other = blocks[n_ctx + at // half][:, lanes]
        return jnp.where(chip == (half - 1 if hop == 1 else 0), other, block)

    def codes_of(rest):
        at = spread * dec_width // LANES
        return rest[at : at + 8, :count]

    for at in range(n_ctx):
        rows = slice(at * count, (at + 1) * count)
        unit, _ = normed_rows(pick(at, tokens_at).astype(F32))
        nrm[rows, :] = (unit * enc_gain[...]).astype(BF16)
        codes = codes_of(pick(at, rest_at).astype(F32))[:1]
        bias[:, rows] = jnp.broadcast_to(jnp.where(codes > 0.5, 0.0, NEG), (8, count))
    loads[0].wait()
    for load in loads[1:]:
        load.start()

    for at in range(3 * groups):
        lanes = slice(at * group_lanes, (at + 1) * group_lanes)
        qkv[:, lanes] = mm(nrm[...], enc_qkv_here[:, lanes]).astype(BF16)
    nrm_t[:PAD, :] = jnp.zeros((PAD, slots), BF16)
    nrm_t[PAD:, :] = nrm[...].T

    def lanes_of(group):
        return [
            pl.ds(pl.multiple_of(at * chans + group * group_lanes, group_lanes), group_lanes)
            for at in range(3)
        ]

    def attend(group, carry):
        lanes, key_lanes, value_lanes = lanes_of(group)
        keys = qkv[:, key_lanes]
        values = qkv[:, value_lanes]
        for head in range(4):
            own = head_lanes(head, chunk, group_lanes)
            for part in range(slots // chunk):
                rows = slice(part * chunk, (part + 1) * chunk)
                query = jnp.where(own, qkv[rows, lanes].astype(F32) * scale, 0.0).astype(BF16)
                scores = mm_nt(query, keys) + bias[:1]
                raised = jnp.exp(scores - jnp.max(scores, axis=-1, keepdims=True))
                share = (raised * (1.0 / jnp.sum(raised, axis=-1, keepdims=True))).astype(BF16)
                weights[group * 4 + head, rows, :] = share
                mix = mm(share, values)
                if head > 0:
                    mix = jnp.where(own, mix, mixed[rows, lanes].astype(F32))
                mixed[rows, lanes] = mix.astype(BF16)
        return carry

    for group in range(groups):
        attend(group, 0)

    loads[1].wait()
    loads[2].wait()
    for at in range(n_ctx):
        rows = slice(at * count, (at + 1) * count)
        out = pick(at, tokens_at).astype(F32) + mm(mixed[rows, :], enc_out_here[...])
        res[rows, :] = out.astype(BF16)
    latent = mm(res[...], enc_to_dec_here[...]).astype(BF16)
    d_latent[...] = latent

    def place(shard, on_core):
        at = shard // 2
        if shard % 2 == 0:
            return at
        return half + (at + on_core) % half

    def rows_of(shard):
        shard = shard % n_ctx
        return slice(shard * count, (shard + 1) * count)

    lane = lax.broadcasted_iota(jnp.int32, (count, LANES), 1).astype(F32)
    square = [lax.broadcasted_iota(jnp.int32, (count, count), axis) for axis in range(2)]
    unity = jnp.where(square[0] == square[1], 1.0, 0.0).astype(BF16)

    def in_time(shard, at):
        dec_in[rows_of(shard), :] = d_latent[rows_of(at), :]
        blk_cot[shard * size : shard * size + count, :] = pick(at, cots_at)
        rest = pick(at, rest_at).astype(F32)
        sums[shard * spread : (shard + 1) * spread, :] = jnp.concatenate(
            [rest[tile * spread : (tile + 1) * spread] for tile in range(dec_width // LANES)], 1
        )
        code = mm_nt(unity, codes_of(rest).astype(BF16))[:, :1] - 1.0
        last = (shard + n_ctx - 1) % n_ctx
        window = code + jnp.where(
            code >= SPOTS, float((shard - 1) * SPOTS), float(last * SPOTS)
        )
        hit = (lane == window) & (code >= 0.0)
        hot[rows_of(shard), :] = jnp.where(hit, 1.0, 0.0).astype(BF16)

    for shard in range(0, n_ctx, 2):
        in_time(shard, place(shard, 0))
    for on_core in range(2):

        @pl.when(core == on_core)
        def _():
            for shard in range(1, n_ctx, 2):
                in_time(shard, place(shard, on_core))

    loads[3].wait()
    loads[4].wait()
    dec_in[slots:, :] = jnp.broadcast_to(mask_token[...], (PAD, dec_width)).astype(BF16)
    for shard in range(n_ctx):
        after = (shard + 1) % n_ctx
        rows_sum = (
            sums[shard * spread + SPOTS : (shard + 1) * spread, :]
            + sums[after * spread : after * spread + SPOTS, :]
        )
        blk_cot[shard * size + count : (shard + 1) * size, :] = jnp.concatenate(
            [rows_sum, jnp.zeros((PAD - SPOTS, dec_width), F32)], 0
        ).astype(BF16)

    dec_unit, dec_scale = normed_rows(dec_in[...].astype(F32))
    dec_nrm = (dec_unit * dec_gain[...]).astype(BF16)
    dec_proj[...] = mm(dec_nrm, dec_qkv_here[...]).astype(BF16)
    d_mixes[...] = mm_nt(blk_cot[...], dec_out_here[...]).astype(BF16)

    pad_row = lax.broadcasted_iota(jnp.int32, (PAD, LANES), 0)
    pad_lane = lax.broadcasted_iota(jnp.int32, (PAD, LANES), 1)
    reach = 3 * count + PAD
    col = lax.broadcasted_iota(jnp.int32, (size, reach), 1)
    owns = [head_lanes(head, size, dec_chans) for head in range(dec_chans // HEAD)]
    tall = len(owns) * size
    mask_rows = slice(slots, slots + PAD)
    query_lanes = slice(0, dec_chans)
    key_lanes = slice(dec_chans, 2 * dec_chans)
    value_lanes = slice(2 * dec_chans, 3 * dec_chans)

    def stack_heads(rows):
        return jnp.concatenate([jnp.where(own, rows, 0.0) for own in owns], 0)

    def unstack_heads(rows):
        total = jnp.where(owns[0], rows[:size], 0.0)
        for head in range(1, len(owns)):
            total = jnp.where(owns[head], rows[head * size : (head + 1) * size], total)
        return total

    def rows_at(shard, rows):
        return pl.ds(pl.multiple_of(shard * rows, PAD), rows)

    def near(ref, shard, lanes, last):
        shards = [lax.rem(shard + n_ctx + step, n_ctx) for step in (-1, 0, 1)]
        return jnp.concatenate([ref[rows_at(at, count), lanes] for at in shards] + [last], 0)

    def keys_of(shard):
        return near(dec_proj, shard, key_lanes, dec_proj[mask_rows, key_lanes])

    def values_of(shard):
        return near(dec_proj, shard, value_lanes, dec_proj[mask_rows, value_lanes])

    def score(shard, here):
        eye = (pad_row + shard * SPOTS == pad_lane) & (pad_row < SPOTS)
        eye = jnp.where(eye, 1.0, 0.0).astype(BF16)
        hot_keys = near(hot, shard, slice(None), jnp.zeros((PAD, LANES), BF16))
        match = mm_nt(jnp.concatenate([hot[rows_at(shard, count), :], eye], 0), hot_keys)
        masked = float(WINDOW) - jnp.sum(match, axis=1, keepdims=True)
        mask_bias = jnp.where(masked > 0.5, jnp.log(jnp.maximum(masked, 1.0)), NEG)
        block_bias = jnp.where(match > 0.5, 0.0, jnp.where(col == 3 * count, mask_bias, NEG))
        queries = jnp.concatenate(
            [dec_proj[rows_at(shard, count), query_lanes], dec_proj[mask_rows, query_lanes]], 0
        )
        queries = stack_heads(queries.astype(F32) * scale).astype(BF16)
        q_stack[here, :] = queries
        d_stack[here, :] = stack_heads(d_mixes[rows_at(shard, size), :].astype(F32)).astype(BF16)
        wide[here, :] = mm_nt(queries, keys_of(shard)) + jnp.concatenate(
            [block_bias] * len(owns), 0
        )

    def soften():
        scores = wide[...]
        raised = jnp.exp(scores - jnp.max(scores, axis=-1, keepdims=True))
        share = raised * (1.0 / jnp.sum(raised, axis=-1, keepdims=True))
        p_stack[...] = share.astype(BF16)

    def mix(shard, here):
        values = values_of(shard)
        blk_mix[rows_at(shard, size), :] = unstack_heads(mm(p_stack[here, :], values)).astype(BF16)
        wide[here, :] = mm_nt(d_stack[here, :], values)

    def soften_back():
        share = p_stack[...].astype(F32)
        d_share = wide[...]
        delta = jnp.sum(d_share * share, axis=-1, keepdims=True)
        d_p_stack[...] = (share * (d_share - delta)).astype(BF16)

    def mix_back(shard, here):
        d_score = d_p_stack[here, :]
        d_query[rows_at(shard, size), :] = unstack_heads(mm(d_score, keys_of(shard))) * scale
        d_keys[shard] = mm_tn(d_score, q_stack[here, :]).astype(BF16)
        d_values[shard] = mm_tn(p_stack[here, :], d_stack[here, :]).astype(BF16)

    at_once = n_ctx

    def some_shards(at, carry):
        both = [(at_once * at + one, slice(one * tall, (one + 1) * tall)) for one in range(at_once)]
        for shard, here in both:
            score(shard, here)
        soften()
        for shard, here in both:
            mix(shard, here)
        soften_back()
        for shard, here in both:
            mix_back(shard, here)
        return carry

    some_shards(0, 0)

    mask_d_query = jnp.zeros((1, dec_chans), F32)
    mask_d_pair = [jnp.zeros((1, dec_chans), F32) for _ in range(2)]
    for shard in range(n_ctx):
        rows = rows_of(shard)
        d_acc[rows, query_lanes] = d_query[shard * size : shard * size + count, :].astype(BF16)
        mask_d_query += jnp.sum(
            d_query[shard * size + count : shard * size + count + SPOTS, :], 0, keepdims=True
        )
        for at, (lanes, ref) in enumerate(((key_lanes, d_keys), (value_lanes, d_values))):
            before, after = (shard + n_ctx - 1) % n_ctx, (shard + 1) % n_ctx
            total = (
                ref[before, 2 * count : 3 * count, :].astype(F32)
                + ref[shard, count : 2 * count, :].astype(F32)
                + ref[after, :count, :].astype(F32)
            )
            d_acc[rows, lanes] = total.astype(BF16)
            mask_d_pair[at] += ref[shard, 3 * count :, :].astype(F32)[:1]
    first = lax.broadcasted_iota(jnp.int32, (PAD, 3 * dec_chans), 0) == 0
    mask_d = jnp.concatenate([mask_d_query] + mask_d_pair, 1)
    d_acc[mask_rows, :] = jnp.where(first, mask_d, 0.0).astype(BF16)

    d_dec_proj = d_acc[...]
    d_dec_nrm = mm_nt(d_dec_proj, dec_qkv_here[...])
    g_dec_qkv = mm_tn(dec_nrm, d_dec_proj)
    g_dec_out = mm_tn(blk_mix[...], blk_cot[...])
    g_dec_gain = jnp.sum(d_dec_nrm * dec_unit, axis=0, keepdims=True)
    d_dec_in = norm_back(d_dec_nrm, dec_unit, dec_scale, dec_gain[...])
    g_mask = jnp.sum(sums[...], axis=0, keepdims=True) + d_dec_in[slots : slots + 1]
    for shard in range(n_ctx):
        cot = blk_cot[shard * size : shard * size + count, :].astype(F32)
        back = d_dec_in[shard * count : (shard + 1) * count].astype(BF16).astype(F32)
        dec_in[rows_of(shard), :] = (cot + back).astype(BF16)
    for on_core in range(2):

        @pl.when(core == on_core)
        def _():
            for shard in range(n_ctx):
                d_latent[rows_of(place(shard, on_core)), :] = dec_in[rows_of(shard), :]

    d_res[...] = mm_nt(d_latent[...], enc_to_dec_here[...]).astype(BF16)
    d_mixed[...] = mm_nt(d_res[...], enc_out_here[...]).astype(BF16)

    places, total = flat_rows(widths)
    block_rows = 2 * total // (n_dp * n_ctx)
    late_at = places[2]

    def store(which, lane_at, grad):
        store_flat(flat, places[which] - late_at, widths[which][1], lane_at, grad)

    store(2, 0, mm_tn(mixed[...], d_res[...]))
    store(3, 0, mm_tn(res[...], d_latent[...]))
    store(4, 0, g_mask)
    store(5, 0, g_dec_gain)
    store(6, 0, g_dec_qkv)
    store(7, 0, g_dec_out)

    def attend_back(group, carry):
        lanes, key_lanes, value_lanes = lanes_of(group)
        turned[:group_lanes, :] = qkv[:, lanes].T
        turned[group_lanes:, :] = d_mixed[:, lanes].T
        keys = qkv[:, key_lanes]
        values = qkv[:, value_lanes]
        for head in range(4):
            own = head_lanes(head, chunk, group_lanes)
            at_head = group * 4 + head
            for part in range(slots // chunk):
                rows = slice(part * chunk, (part + 1) * chunk)
                cot = jnp.where(own, d_mixed[rows, lanes].astype(F32), 0.0)
                delta = jnp.sum(cot * mixed[rows, lanes].astype(F32), axis=-1, keepdims=True)
                d_share = mm_nt(cot.astype(BF16), values)
                d_score = weights[at_head, rows, :].astype(F32) * (d_share - delta)
                d_score = d_score.astype(BF16)
                d_scores[head % 2, rows, :] = d_score
                d_query = mm(d_score, keys) * scale
                if head > 0:
                    d_query = jnp.where(own, d_query, d_qkv[rows, lanes].astype(F32))
                d_qkv[rows, lanes] = d_query.astype(BF16)
            to_key = pl.ds(pl.multiple_of(at_head * HEAD, HEAD), HEAD)
            to_value = pl.ds(pl.multiple_of(chans + at_head * HEAD, HEAD), HEAD)
            query_t = turned[head * HEAD : (head + 1) * HEAD, :]
            cot_t = turned[group_lanes + head * HEAD : group_lanes + (head + 1) * HEAD, :]
            d_kv_t[to_key, :] = (mm(query_t, d_scores[head % 2]) * scale).astype(BF16)
            d_kv_t[to_value, :] = mm(cot_t, weights[at_head]).astype(BF16)
        return carry

    for group in range(groups):
        attend_back(group, 0)
    d_qkv[:, chans:] = d_kv_t[...].T

    d_nrm = mm_nt(d_qkv[...], enc_qkv_here[...])
    gain_grad = jnp.sum(d_nrm * nrm[...].astype(F32), axis=0, keepdims=True) / enc_gain[...]
    unit, unit_scale = normed_rows(blocks[0][:, tokens_at].astype(F32))
    d_own = norm_back(d_nrm[:count], unit, unit_scale, enc_gain[...]).astype(BF16).astype(F32)
    d_patches[...] = (d_res[:count, :].astype(F32) + d_own).astype(BF16)

    piece_rows = cut.shape[1]
    some = head_rows(widths, n_dp, n_ctx)
    lanes_all = 3 * chans
    tiles = lanes_all // LANES

    def cut_at(ref, start, to):
        slot = to ^ dp_at if n_dp & (n_dp - 1) == 0 else lax.rem(to - dp_at + n_dp, n_dp)
        shift = lax.rem(start, 8)
        base = start - shift
        for small in range(8):

            @pl.when(shift == small)
            def _():
                rows = ref[pl.ds(pl.multiple_of(base, 8), piece_rows + 8), :]
                cut[slot] = rows[small : small + piece_rows].astype(BF16)

    def cut_early(to, carry):
        start = (to * n_ctx + ctx_at) * block_rows // 2
        first = (start - places[1] + PAD * tiles) // tiles // PAD * PAD
        rows = nrm_t[pl.ds(pl.multiple_of(first, PAD), some), :]
        store_flat(part, 0, lanes_all, 0, mm(rows, d_qkv[...]))
        begin = start - places[1] + (PAD - first) * tiles

        @pl.when(start == 0)
        def _():
            store_flat(part, PAD * tiles - places[1], width, 0, gain_grad)

        cut_at(part, begin, to)
        return carry

    def cut_late(to, carry):
        cut_at(flat, (to * n_ctx + ctx_at) * block_rows // 2 - late_at, to)
        return carry

    first_late = late_at * n_dp // total
    lax.fori_loop(0, first_late, cut_early, 0)
    lax.fori_loop(first_late, n_dp, cut_late, 0)
    for at in range(n_dp):
        pieces[at][...] = cut[at]


def join_kernel(*refs):
    out = refs[-1]
    total = refs[0][...].astype(F32)
    for ref in refs[1:-1]:
        total = total + ref[...].astype(F32)
    rows = total.shape[0]
    lane = lax.broadcasted_iota(jnp.int32, (rows, LANES), 1)
    turned = pltpu.roll(total, LANES // 2, 1)
    turned = jnp.where(lane < LANES // 2, turned, pltpu.roll(turned, rows - 1, 0))
    total = jnp.where(lax.rem(lax.axis_index("ctx"), 2) == 1, turned, total)
    full = out.shape[0] // (8 * LANES) * 8
    left = out.shape[0] - full * LANES
    out[: full * LANES] = total[:full].reshape(full * LANES)
    if left > 0:
        out[full * LANES :] = total[full : full + 8].reshape(8 * LANES)[:left]


def fused_body(
    n_dp,
    n_ctx,
    patches,
    vis_index,
    shifts,
    enc_gain,
    enc_qkv,
    enc_out,
    enc_to_dec,
    mask_token,
    dec_gain,
    dec_qkv,
    dec_out,
    dec_cot,
):
    tokens = patches[0]
    params = (enc_gain, enc_qkv, enc_out, enc_to_dec, mask_token, dec_gain, dec_qkv, dec_out)
    widths = [(1,) * (2 - param.ndim) + param.shape for param in params]
    half = n_ctx // 2

    def by_hops(block):
        def shift(array, hops, chips):
            pairs = [((chip + hops) % half, chip) for chip in chips]
            turn = [(2 * pair[0] + core, 2 * pair[1] + core) for pair in pairs for core in range(2)]
            return lax.ppermute(array, "ctx", turn)

        def swap(array, chips):
            return lax.ppermute(
                array, "ctx", [(2 * chip + core, 2 * chip + 1 - core) for chip in chips for core in range(2)]
            )

        every = range(half)
        if half != 4:
            near = [block] + [shift(block, step, every) for step in range(1, half)]
            return near + [swap(other, every) for other in near]
        where = (every, every[:-1], every, every[1:], (0, half - 1))
        middle = shift(block, 2, every)
        first, last = shift(block, 1, where[1]), shift(block, 3, where[3])
        ends = lax.ppermute(
            middle, "ctx", [(2 * a + core, 2 * b + core) for a, b in ((1, 0), (2, 3)) for core in range(2)]
        )
        near = [block, first, middle, last, ends]
        far = [swap(other, chips) for other, chips in zip(near, where)]
        return near[:4] + far[:4] + [near[4], far[4]]

    blocks = by_hops(call_pack(shifts, tokens, vis_index, dec_cot[0]))
    d_patches, *pieces = call_clip(n_dp, n_ctx, widths, blocks, params)
    got = [pieces[0]]
    for step in range(1, n_dp):
        if n_dp & (n_dp - 1) == 0:
            turn = [(at, at ^ step) for at in range(n_dp)]
        else:
            turn = [(at, (at + step) % n_dp) for at in range(n_dp)]
        got.append(lax.ppermute(pieces[step], "dp", turn))
    share = flat_rows(widths)[1] * LANES // (n_dp * n_ctx)
    return d_patches[None], call_join(got, share)


def piece_shape(n_dp, n_ctx, widths):
    share = flat_rows(widths)[1] * LANES // (n_dp * n_ctx)
    rows = -(-(share + LANES // 2) // LANES)
    return jax.ShapeDtypeStruct((-(-rows // PAD) * PAD, LANES), BF16)


IN_VMEM = pl.BlockSpec(memory_space=pltpu.VMEM)
IN_SMEM = pl.BlockSpec(memory_space=pltpu.SMEM)
ANYWHERE = pl.BlockSpec(memory_space=pl.ANY)


def call_pack(shifts, tokens, vis_index, cot):
    count, width = tokens.shape
    return pl.pallas_call(
        pack_kernel,
        out_shape=jax.ShapeDtypeStruct((count, width + cot.shape[1] + LANES), BF16),
        in_specs=[IN_SMEM, IN_VMEM, IN_VMEM, IN_VMEM],
        out_specs=IN_VMEM,
        name="pack",
    )(shifts, tokens, vis_index, cot)


def call_clip(n_dp, n_ctx, widths, blocks, params):
    enc_gain, enc_qkv, enc_out, enc_to_dec, mask_token, dec_gain, dec_qkv, dec_out = params
    count, width = blocks[0].shape[0], enc_gain.shape[0]
    slots = n_ctx * count
    chans = enc_out.shape[0]
    dec_chans, dec_width = dec_out.shape
    places, total = flat_rows(widths)
    piece = piece_shape(n_dp, n_ctx, widths)
    part_rows = (head_rows(widths, n_dp, n_ctx) + PAD) * 3 * chans // LANES + 2 * PAD
    size = count + PAD
    tall = dec_chans // HEAD * size
    reach = 3 * count + PAD
    matrices = (enc_qkv, enc_out, enc_to_dec, dec_qkv, dec_out)
    return pl.pallas_call(
        functools.partial(clip_kernel, n_dp, n_ctx, len(blocks), widths),
        out_shape=[jax.ShapeDtypeStruct((count, width), BF16)] + [piece] * n_dp,
        in_specs=[IN_VMEM] * (len(blocks) + 3) + [ANYWHERE] * len(matrices),
        out_specs=[IN_VMEM] * (1 + n_dp),
        scratch_shapes=[
            pltpu.VMEM((slots, width), BF16),
            pltpu.VMEM((PAD + width, slots), BF16),
            pltpu.VMEM((slots, 3 * chans), BF16),
            pltpu.VMEM((chans // HEAD, slots, slots), BF16),
            pltpu.VMEM((slots, chans), BF16),
            pltpu.VMEM((slots, width), BF16),
            pltpu.VMEM((slots + PAD, dec_width), BF16),
            pltpu.VMEM((slots + PAD, 3 * dec_chans), BF16),
            pltpu.VMEM((slots, LANES), BF16),
            pltpu.VMEM((n_ctx * 2 * SPOTS, dec_width), F32),
            pltpu.VMEM((n_ctx * size, dec_chans), BF16),
            pltpu.VMEM((slots + PAD, 3 * dec_chans), BF16),
            pltpu.VMEM((n_ctx * size, dec_chans), BF16),
            pltpu.VMEM((n_ctx * size, dec_width), BF16),
            pltpu.VMEM((n_ctx * tall, reach), F32),
            pltpu.VMEM((n_ctx * tall, dec_chans), BF16),
            pltpu.VMEM((n_ctx * tall, dec_chans), BF16),
            pltpu.VMEM((n_ctx * tall, reach), BF16),
            pltpu.VMEM((n_ctx * tall, reach), BF16),
            pltpu.VMEM((n_ctx * size, dec_chans), F32),
            pltpu.VMEM((n_ctx, reach, dec_chans), BF16),
            pltpu.VMEM((n_ctx, reach, dec_chans), BF16),
            pltpu.VMEM((slots, dec_width), BF16),
            pltpu.VMEM((slots, width), BF16),
            pltpu.VMEM((slots, chans), BF16),
            pltpu.VMEM((8 * HEAD, slots), BF16),
            pltpu.VMEM((2, slots, slots), BF16),
            pltpu.VMEM((2 * chans, slots), BF16),
            pltpu.VMEM((slots, 3 * chans), BF16),
            pltpu.VMEM((8, slots), F32),
        ]
        + [pltpu.VMEM(matrix.shape, BF16) for matrix in matrices]
        + [
            pltpu.VMEM((total - places[2] + 2 * PAD, LANES), F32),
            pltpu.VMEM((part_rows, LANES), F32),
            pltpu.VMEM((n_dp,) + piece.shape, BF16),
            pltpu.SemaphoreType.DMA((len(matrices),)),
        ],
        compiler_params=pltpu.CompilerParams(vmem_limit_bytes=VMEM_BYTES),
        cost_estimate=pl.CostEstimate(
            flops=40 * 10**9, bytes_accessed=16 * 2**20, transcendentals=0
        ),
        name="clip",
    )(
        *blocks,
        enc_gain[None],
        mask_token[None],
        dec_gain[None],
        *matrices,
    )


def call_join(blocks, share):
    return pl.pallas_call(
        join_kernel,
        out_shape=jax.ShapeDtypeStruct((share,), F32),
        in_specs=[IN_VMEM] * len(blocks),
        out_specs=IN_VMEM,
        compiler_params=pltpu.CompilerParams(vmem_limit_bytes=SMALL_VMEM_BYTES),
        name="join",
    )(*blocks)


SMALL_VMEM_BYTES = 8 * 1024 * 1024
VMEM_BYTES = 56 * 1024 * 1024


def body(n_dp, n_ctx, patches, vis_index, *rest):
    enc_qkv = rest[2]
    dec_cot = rest[-1]
    head = enc_qkv.shape[0] * (1 + enc_qkv.shape[1])
    length = sum(param.size for param in rest[1:-1])
    small = n_ctx * patches.shape[1] <= FUSED_SLOTS
    whole = head * n_dp % length == 0 and dec_cot.shape[1] == WT * CELLS
    if small and n_ctx % 2 == 0 and whole:
        return fused_body(n_dp, n_ctx, patches, vis_index, *rest)
    return plain_body(patches, vis_index, *rest)


def solution(mesh):
    in_specs = (
        P("dp", "ctx", None),
        P("dp", "ctx"),
        P("dp", None),
        P(),
        P(),
        P(),
        P(),
        P(),
        P(),
        P(),
        P(),
        P("dp", "ctx", None),
    )
    out_specs = (P("dp", "ctx", None), P(("dp", "ctx")))
    return jax.shard_map(functools.partial(body, mesh.shape["dp"], mesh.shape["ctx"]), mesh=mesh, in_specs=in_specs, out_specs=out_specs, check_vma=False)
```
